128 devices in a mesh: dp: 8 (over y, x_hi), graph: 16 (over x_lo, z, core).
Axes of the slice: x: 4 (x_hi: 2, x_lo: 2; x = x_hi * 2 + x_lo), y: 4, z: 4, core: 2. Of those that a mesh axis runs over, the one named last changes fastest.
Arguments:
- node_state: bfloat16 [8, 14336, 128], P('dp', 'graph'), may hold values from -6 to 6
- atom_types: int32 [8, 14336], P('dp', 'graph'), may hold values from 0 to 89
- positions: float32 [8, 3, 14336], P('dp', None, 'graph'), may hold values from 0 to 6
- force_ref: float32 [8, 3, 14336], P('dp', None, 'graph'), may hold values from -8 to 8
- edge_source: int32 [8, 286720], P('dp', 'graph'), may hold values from 0 to 14335, as said below
- edge_count: int32 [8, 16], P('dp', 'graph'), may hold values from 8960 to 17920, as said below
- type_table: bfloat16 [90, 128], replicated, may hold values from -3 to 3
- w_rad: bfloat16 [256, 128], replicated, may hold values from -3 to 3
- w_src: bfloat16 [128, 128], replicated, may hold values from -0.5 to 0.5
- w_out: float32 [128], replicated, may hold values from -0.06 to 0.06
Outputs:
- forces: float32 [8, 3, 14336], P('dp', None, 'graph')
- grad_radial: float32 [256, 128], replicated
- grad_source: float32 [128, 128], replicated
- grad_out: float32 [128], replicated
- loss: float32 [], replicated
The draws below stay inside these ranges and needn't reach their ends.
Inputs may be any that keep to these rules, and one draw needn't show every extreme that they name: `edge_source`: of the slots of block k (slots k*17920 to (k+1)*17920 - 1), the first 2240 name a source node of the block half the number of blocks away from k, taken around; every other slot names a source node of block k-1, k or k+1, taken around the ends, and never its own target node (slot e // 20); blocks hold 896 nodes each. `edge_count`: in every batch some block has all 17920 slots live.
All inputs are finite; a program needn't handle non-finite values.
Results may differ from the reference program's by a relative error of at most 0.0049.
Values may be sent and summed in bfloat16 or wider, within the bound.
A program may use at most 192 MiB of HBM per device.

```python
import math
import jax
import jax.numpy as jnp
from jax import lax

C = 128
K = 256
TYPES = 90
DEG = 20
NB = 896
EDGE_DEV = 17920
NODES = 14336
EDGES = 286720
BATCHES = 8


def draw_edge_source(key, part):
    key = jax.random.fold_in(key, 3)
    groups = EDGES // EDGE_DEV
    slots = jnp.arange(EDGES, dtype=jnp.int32)[None, :]
    block = slots // EDGE_DEV
    far_slot = slots % EDGE_DEV < EDGE_DEV // 8
    second_key, third_key = jax.random.split(key)
    target = jnp.broadcast_to(slots // DEG, (BATCHES, EDGES))
    step = jax.random.randint(second_key, (BATCHES, EDGES), -1, 2)
    step = jnp.where(far_slot, groups // 2, step)
    source_block = (block + step + groups) % groups
    source_local = jax.random.randint(third_key, (BATCHES, EDGES), 0, NB)
    source = source_block * NB + source_local
    source = jnp.where(source == target, source_block * NB + (source_local + 1) % NB, source)
    return source.astype(jnp.int32)


def draw_edge_count(key, part):
    key = jax.random.fold_in(key, 7)
    groups = EDGES // EDGE_DEV
    count_key, full_key = jax.random.split(key)
    counts = jax.random.randint(count_key, (BATCHES, groups), EDGE_DEV // 2, EDGE_DEV + 1)
    full = jax.random.randint(full_key, (BATCHES, 1), 0, groups)
    blocks = jnp.arange(groups, dtype=jnp.int32)[None, :]
    return jnp.where(blocks == full, EDGE_DEV, counts).astype(jnp.int32)


def plant(entries, key, smallest, high):
    longest = entries.shape.index(max(entries.shape))
    spots = []
    for shift in (0, 1):
        where = [jax.random.randint(jax.random.fold_in(key, axis), (), 0, length) for axis, length in enumerate(entries.shape)]
        where[longest] = (where[longest] + shift) % entries.shape[longest]
        spots.append(tuple(where))
    return entries.at[spots[0]].set(smallest).at[spots[1]].set(high)


def level_of(own_key, extent, cuts, smallest, top_value):
    level = 1.0
    for position, parts in cuts:
        heights = jax.random.uniform(jax.random.fold_in(jax.random.fold_in(own_key, 6), position), (parts,), jnp.float32, smallest / len(cuts), top_value / len(cuts))
        level = level * jnp.repeat(jnp.exp(heights), extent[position] // parts).reshape((-1,) + (1,) * (len(extent) - 1 - position))
    return level


def gaussian(own_key, dims, deviation, limit, shards=(), kind=jnp.bfloat16):
    array = jax.random.normal(own_key, dims, jnp.float32) * deviation
    if len(shards) > 0:
        array = level_of(own_key, dims, shards, -0.22, 0.18) * array
    return jnp.clip(array, min=-limit, max=limit).astype(kind)


def setup_inputs(seed: int = 0) -> dict:
    splits = jax.random.split(jax.random.key(seed), 11)
    node_state = gaussian(splits[0], (BATCHES, NODES, C), 1.0, 6.0, ((0, 8), (1, 16)))
    atom_types = plant(jax.random.randint(splits[1], (BATCHES, NODES), 0, TYPES), jax.random.fold_in(splits[1], 1), 0, TYPES - 1).astype(jnp.int32)
    positions = jnp.clip(6.0 * jax.random.uniform(splits[2], (BATCHES, 3, NODES), jnp.float32) ** level_of(splits[2], (BATCHES, 3, NODES), ((0, 8), (2, 16)), -0.2, 0.2), 0.0, 6.0)
    force_ref = gaussian(splits[3], (BATCHES, 3, NODES), 1.5, 8.0, ((0, 8), (2, 16)), jnp.float32)
    edge_source = draw_edge_source(jax.random.fold_in(splits[10], 71), 0)
    edge_count = draw_edge_count(jax.random.fold_in(splits[10], 71), 0)
    type_table = gaussian(splits[6], (TYPES, C), 0.5, 3.0)
    w_rad = gaussian(splits[7], (K, C), 0.5, 3.0)
    w_src = gaussian(splits[8], (C, C), C ** -0.5, 0.5)
    w_out = gaussian(splits[9], (C,), 0.01, 0.06, (), jnp.float32)
    return dict(node_state=node_state, atom_types=atom_types, positions=positions, force_ref=force_ref, edge_source=edge_source, edge_count=edge_count, type_table=type_table, w_rad=w_rad, w_src=w_src, w_out=w_out)


def basis(dist):
    centers = jnp.arange(K, dtype=jnp.float32) * (12.0 / K)
    gamma = K * K / 1152.0
    diff = dist[:, None] - centers[None, :]
    bump = jnp.exp(-gamma * diff * diff)
    return (bump.astype(jnp.bfloat16), (-2.0 * gamma * diff * bump).astype(jnp.bfloat16))

def derivatives(agg):
    sig = jax.nn.sigmoid(agg)
    first = sig * (1.0 + agg * (1.0 - sig))
    second = sig * (1.0 - sig) * (2.0 + agg * (1.0 - 2.0 * sig))
    return (first, second)

def reference(node_state, atom_types, positions, force_ref, edge_source, edge_count, type_table, w_rad, w_src, w_out):
    weight_loss = 1.0 / math.sqrt(3.0 * NODES * BATCHES)
    target = (jnp.arange(EDGES, dtype=jnp.int32) // DEG).astype(jnp.int32)

    def one_batch(items):
        feats, kinds, places, wanted, source, counts = items
        state = (feats.astype(jnp.float32) + type_table[kinds].astype(jnp.float32)).astype(jnp.bfloat16)
        slots = jnp.arange(EDGES, dtype=jnp.int32)
        live = (slots % EDGE_DEV < counts[slots // EDGE_DEV]).astype(jnp.float32)
        delta = places[:, source] - places[:, target]
        dist = jnp.sqrt(lax.optimization_barrier(jnp.sum(delta * delta, axis=0)) + 0.25)
        unit = delta / dist
        rbf, drbf = basis(dist)
        radial = jnp.dot(rbf, w_rad, preferred_element_type=jnp.float32)
        slope = jnp.dot(drbf, w_rad, preferred_element_type=jnp.float32)
        source_rows = state[source]
        query = jnp.dot(source_rows, w_src, preferred_element_type=jnp.float32)
        agg = 0.2 * jax.ops.segment_sum(live[:, None] * radial * query, target, num_segments=NODES)
        first, second = derivatives(agg)
        readout = first * w_out
        pull = 0.2 * live * lax.optimization_barrier(jnp.sum(readout[target] * query * slope, axis=1))
        moved = (pull[None, :] * unit).T
        forces = (jax.ops.segment_sum(moved, target, num_segments=NODES) - jax.ops.segment_sum(moved, source, num_segments=NODES)).T
        miss = forces - wanted
        loss_part = weight_loss * jnp.sum(miss * miss)
        back = 2.0 * weight_loss * miss
        lam = live * lax.optimization_barrier(jnp.sum((back[:, target] - back[:, source]) * unit, axis=0))
        over_slope = 0.2 * lam[:, None] * readout[target]
        dread = 0.2 * jax.ops.segment_sum(lam[:, None] * query * slope, target, num_segments=NODES)
        grad_out_part = lax.optimization_barrier(jnp.sum(dread * first, axis=0))
        over_plain = 0.2 * live[:, None] * (dread * w_out * second)[target]
        coef_plain = (over_plain * query).astype(jnp.bfloat16)
        coef_slope = (over_slope * query).astype(jnp.bfloat16)
        dquery = (over_slope * slope + over_plain * radial).astype(jnp.bfloat16)
        grad_radial_part = jnp.dot(rbf.T, coef_plain, preferred_element_type=jnp.float32) + jnp.dot(drbf.T, coef_slope, preferred_element_type=jnp.float32)
        grad_source_part = jnp.dot(source_rows.T, dquery, preferred_element_type=jnp.float32)
        return (forces, grad_radial_part, grad_source_part, grad_out_part, loss_part)
    forces, grad_radial, grad_source, grad_out, loss = lax.map(one_batch, (node_state, atom_types, positions, force_ref, edge_source, edge_count))
    return (forces, lax.optimization_barrier(jnp.sum(grad_radial, axis=0)), lax.optimization_barrier(jnp.sum(grad_source, axis=0)), lax.optimization_barrier(jnp.sum(grad_out, axis=0)), jnp.sum(loss))
```

```python
import functools
import math

import jax
import jax.numpy as jnp
from jax import lax
from jax.experimental import pallas as pl
from jax.experimental.pallas import tpu as pltpu
from jax.sharding import PartitionSpec as P

MESH = pl.DeviceIdType.MESH
F32 = jnp.float32
BF16 = jnp.bfloat16
NT = (((1,), (1,)), ((), ()))
DEG = 20
PAD = 24
LANES = 128
VMEM = pltpu.VMEM
LIMIT = 56 * 1024 * 1024


def partners(groups):
    me = lax.axis_index("graph")
    left = lax.rem(me + groups - 1, groups)
    right = lax.rem(me + 1, groups)
    far = lax.rem(me + groups // 2, groups)
    return left, right, far


def greet(devices):
    barrier = pltpu.get_barrier_semaphore()
    for device in devices:
        pl.semaphore_signal(barrier, inc=1, device_id=device, device_id_type=MESH)
    pl.semaphore_wait(barrier, len(devices))


def send(src, dst, send_sem, recv_sem, device):
    copy = pltpu.make_async_remote_copy(
        src_ref=src,
        dst_ref=dst,
        send_sem=send_sem,
        recv_sem=recv_sem,
        device_id=device,
        device_id_type=MESH,
    )
    copy.start()
    return copy


def halo_kernel(
    groups,
    state_ref,
    types_ref,
    place_ref,
    table_ref,
    out_state,
    out_place,
    own_state,
    own_place,
    send_sem,
    recv_sem,
    local_sem,
):
    nodes = state_ref.shape[0]
    kinds = table_ref.shape[0]
    left, right, far = partners(groups)
    targets = ((left, 2), (right, 0), (far, 3))
    own_place[...] = jnp.zeros_like(own_place)
    for c in range(3):
        for n in range(nodes // LANES):
            own_place[8 * c + n : 8 * c + n + 1, :] = place_ref[c : c + 1, n * LANES : (n + 1) * LANES]
    onehot = (
        types_ref[...] == lax.broadcasted_iota(jnp.int32, (kinds, nodes), 0)
    ).astype(BF16)
    embedded = lax.dot_general(
        table_ref[...], onehot, (((0,), (0,)), ((), ())), preferred_element_type=F32
    )
    own_state[...] = (state_ref[...].astype(F32).T + embedded).astype(BF16)
    greet([{"graph": left}, {"graph": right}, {"graph": far}])
    copies = []
    for i, (device, slot) in enumerate(targets):
        copies.append(
            send(own_state, out_state.at[slot], send_sem.at[i], recv_sem.at[i], {"graph": device})
        )
        copies.append(
            send(own_place, out_place.at[slot], send_sem.at[3 + i], recv_sem.at[3 + i], {"graph": device})
        )
    first = pltpu.make_async_copy(own_state, out_state.at[1], local_sem.at[0])
    second = pltpu.make_async_copy(own_place, out_place.at[1], local_sem.at[1])
    first.start()
    second.start()
    for copy in copies:
        copy.wait()
    first.wait()
    second.wait()


def lane_pick(row, index):
    return jnp.take_along_axis(
        jnp.broadcast_to(row, index.shape), index, axis=1, mode="promise_in_bounds"
    )


def pick_three(tab_ref, rows, lane, row_of):
    result = [jnp.zeros(lane.shape, F32)] * 3
    for r in range(rows):
        here = row_of == r
        for c in range(3):
            at = (r // 7) * PAD + c * 8 + r % 7
            result[c] = jnp.where(here, lane_pick(tab_ref[at : at + 1, :], lane), result[c])
    return result


def basis(dist_row, scaled_centers, gamma):
    diff = (-2.0 * gamma) * dist_row - scaled_centers
    bump = jnp.exp2(diff * diff * (-math.log2(math.e) / (4.0 * gamma)))
    return bump.astype(BF16), (diff * bump).astype(BF16)


def centers(count):
    gamma = count * count / 1152.0
    number = lax.broadcasted_iota(jnp.int32, (count, LANES), 0).astype(F32)
    return number * (12.0 / count) * (-2.0 * gamma), gamma


def node_terms(agg):
    sig = jax.nn.sigmoid(agg)
    first = sig * (1.0 + agg * (1.0 - sig))
    second = sig * (1.0 - sig) * (2.0 + agg * (1.0 - 2.0 * sig))
    return first, second


STEP = 4


def forward_kernel(
    groups,
    state_ref,
    place_ref,
    source_ref,
    count_ref,
    w_rad_ref,
    w_src_ref,
    w_out_ref,
    rows_ref,
    query_ref,
    slope_ref,
    radial_ref,
    scalar_ref,
    index_ref,
    agg_ref,
    incoming_ref,
    outgoing_ref,
    stack,
    w_rad_t,
    w_src_t,
    w_out_t,
    centre,
    pick,
    onehots,
    product,
    agg_acc,
    spread,
):
    n = pl.program_id(0)
    channels = w_src_ref.shape[0]
    count = w_rad_ref.shape[0]
    gamma = count * count / 1152.0
    me = lax.axis_index("graph")

    @pl.when(n == 0)
    def _():
        w_rad_t[...] = w_rad_ref[...].astype(F32).T.astype(BF16)
        w_src_t[...] = w_src_ref[...].astype(F32).T.astype(BF16)
        w_out_t[...] = jnp.broadcast_to(w_out_ref[...], (channels, LANES)).T
        centre[...] = centers(count)[0]
        spread[...] = jnp.zeros_like(spread)
        incoming_ref[...] = jnp.zeros_like(incoming_ref)
        for half in range(28):
            rows = slice((half // 2) * channels, (half // 2 + 1) * channels)
            at = (half % 7) * LANES
            stack[rows, (half % 2) * LANES : (half % 2 + 1) * LANES] = state_ref[
                half // 7, :, at : at + LANES
            ]

    slot = lax.broadcasted_iota(jnp.int32, (PAD, LANES), 1) * DEG + lax.broadcasted_iota(
        jnp.int32, (PAD, LANES), 0
    )
    lane = slot & (LANES - 1)
    row_of = slot >> 7
    source = jnp.zeros((PAD, LANES), jnp.int32)
    for r in range(DEG):
        source = jnp.where(row_of == r, lane_pick(source_ref[pl.ds(n * DEG + r, 1), :], lane), source)
    nodes = 7 * LANES
    block = (source * 74899) >> 26
    offset = (block - me + groups) & (groups - 1)
    position = jnp.where(
        offset == groups - 1, 0, jnp.where(offset == 0, 1, jnp.where(offset == 1, 2, 3))
    )
    picked = position * nodes + source - block * nodes
    live = slot + n * (DEG * LANES) < count_ref[0, 0]
    lane = picked & (LANES - 1)
    row_of = picked >> 7
    index_ref[0, :PAD] = lane
    index_ref[0, PAD:] = row_of
    source_place = pick_three(place_ref, 28, lane, row_of)
    delta = [
        source_place[c] - place_ref[pl.ds(PAD + 8 * c + n, 1), :] for c in range(3)
    ]
    dist = jnp.sqrt(delta[0] * delta[0] + delta[1] * delta[1] + delta[2] * delta[2] + 0.25)
    unit = [delta[c] / dist for c in range(3)]
    for c in range(3):
        scalar_ref[0, c * PAD : (c + 1) * PAD] = unit[c]
    scalar_ref[0, 3 * PAD :] = dist
    pick[:PAD] = jnp.where(live, (picked & 255).astype(F32), -1.0)
    pick[PAD : 2 * PAD] = (picked >> 8).astype(F32)
    pick[2 * PAD :] = dist
    agg_acc[...] = jnp.zeros_like(agg_acc)
    wide = STEP * LANES

    def piece(i, chunks):
        place = pl.ds(pl.multiple_of(i * wide, wide), wide)
        numbers = lax.broadcasted_iota(jnp.int32, (256, LANES), 0).astype(F32)
        ones, bumps, slants, hi = [], [], [], []
        for j in range(STEP):
            column = pick[pl.ds(i * STEP + j, 1), :]
            ones.append((numbers == column).astype(BF16))
            bump, slant = basis(pick[pl.ds(2 * PAD + i * STEP + j, 1), :], centre[...], gamma)
            bumps.append(bump)
            slants.append(slant)
            hi.append(pick[pl.ds(PAD + i * STEP + j, 1), :])
        ones = jnp.concatenate(ones, axis=1)
        bumps = jnp.concatenate(bumps, axis=1)
        slants = jnp.concatenate(slants, axis=1)
        hi = jnp.broadcast_to(jnp.concatenate(hi, axis=1), (channels, wide))
        onehots[:, place] = ones
        found = jnp.dot(stack[: chunks * channels], ones, preferred_element_type=F32)
        rows = found[:channels]
        for c in range(1, chunks):
            rows = jnp.where(hi == float(c), found[c * channels : (c + 1) * channels], rows)
        rows = rows.astype(BF16)
        rows_ref[0, :, place] = rows
        query = jnp.dot(w_src_t[...], rows, preferred_element_type=F32)
        radial = jnp.dot(w_rad_t[...], bumps, preferred_element_type=F32)
        slope = jnp.dot(w_rad_t[...], slants, preferred_element_type=F32)
        query_ref[0, :, place] = query.astype(BF16)
        slope_ref[0, :, place] = slope.astype(BF16)
        radial_ref[0, :, place] = radial.astype(BF16)
        product[:, place] = query * slope
        term = radial * query
        total = term[:, :LANES]
        for j in range(1, STEP):
            total = total + term[:, j * LANES : (j + 1) * LANES]
        agg_acc[...] += total

    @pl.when(n == 0)
    def _():
        lax.fori_loop(0, DEG // STEP, lambda i, u: (piece(i, 14), u)[1], 0)

    @pl.when(n > 0)
    def _():
        lax.fori_loop(0, DEG // STEP, lambda i, u: (piece(i, 11), u)[1], 0)

    agg = 0.2 * agg_acc[...]
    agg_ref[0] = agg
    first, _ = node_terms(agg)
    readout = 0.2 * first * w_out_t[...]
    incoming = [jnp.zeros((1, LANES), F32)] * 3
    lhs = []
    chunk = lax.broadcasted_iota(jnp.int32, (16, LANES), 0).astype(F32)
    for j in range(DEG):
        pull = jnp.sum(readout * product[:, j * LANES : (j + 1) * LANES], axis=0, keepdims=True)
        here = chunk == pick[PAD + j : PAD + j + 1, :]
        high, low = [], []
        for c in range(3):
            moved = pull * scalar_ref[0, c * PAD + j : c * PAD + j + 1, :]
            incoming[c] = incoming[c] + moved
            term = jnp.where(here, moved, 0.0)
            top = term.astype(BF16)
            high.append(top)
            low.append((term - top.astype(F32)).astype(BF16))
        lhs.append(jnp.concatenate(high + low, axis=0))
    lhs = jnp.concatenate(lhs, axis=1)
    spread[...] += lax.dot_general(lhs, onehots[...], NT, preferred_element_type=F32)
    for c in range(3):
        incoming_ref[pl.ds(8 * c + n, 1), :] = incoming[c]

    @pl.when(n == 6)
    def _():
        outgoing_ref[...] = jnp.zeros_like(outgoing_ref)
        total = spread[:48] + spread[48:]
        for c in range(3):
            for r in range(28):
                at = (r // 7) * PAD + c * 8 + r % 7
                outgoing_ref[at : at + 1, :] = total[
                    c * 16 + r // 2 : c * 16 + r // 2 + 1, (r % 2) * LANES : (r % 2 + 1) * LANES
                ]


def force_kernel(
    groups,
    weight_loss,
    outgoing_ref,
    incoming_ref,
    wanted_ref,
    forces_ref,
    back_ref,
    loss_ref,
    terms,
    mine,
    wanted,
    tables,
    send_sem,
    recv_sem,
):
    left, right, far = partners(groups)
    greet([{"graph": left}, {"graph": right}, {"graph": far}])
    copies = []
    for i, (device, slot) in enumerate(((left, 0), (right, 2), (far, 3))):
        copies.append(
            send(
                outgoing_ref.at[slot * PAD : (slot + 1) * PAD],
                terms.at[i],
                send_sem.at[i],
                recv_sem.at[i],
                {"graph": device},
            )
        )
    wanted[...] = jnp.zeros_like(wanted)
    for c in range(3):
        for n in range(7):
            wanted[8 * c + n : 8 * c + n + 1, :] = wanted_ref[c : c + 1, n * LANES : (n + 1) * LANES]
    for copy in copies:
        copy.wait()
    forces = incoming_ref[...] - (outgoing_ref[PAD : 2 * PAD] + terms[0] + terms[1] + terms[2])
    miss = forces - wanted[...]
    mine[...] = 2.0 * weight_loss * miss
    copies = []
    for i, device in enumerate((left, right, far)):
        copies.append(
            send(mine, tables.at[i], send_sem.at[3 + i], recv_sem.at[3 + i], {"graph": device})
        )
    for c in range(3):
        for n in range(7):
            forces_ref[c : c + 1, n * LANES : (n + 1) * LANES] = forces[8 * c + n : 8 * c + n + 1, :]
    square = miss * miss
    total = weight_loss * jnp.sum(square, axis=(0, 1), keepdims=True)
    loss_ref[...] = jnp.broadcast_to(total, loss_ref.shape)
    back_ref[PAD : 2 * PAD] = mine[...]
    for copy in copies:
        copy.wait()
    back_ref[2 * PAD : 3 * PAD] = tables[0]
    back_ref[:PAD] = tables[1]
    back_ref[3 * PAD :] = tables[2]


def backward_kernel(
    back_ref,
    scalar_ref,
    index_ref,
    agg_ref,
    rows_ref,
    query_ref,
    slope_ref,
    radial_ref,
    w_out_ref,
    grads_ref,
    w_out_t,
    centre,
    lam_ref,
    coefs,
    bases,
    wants,
    grad_radial,
    grad_source,
    grad_out,
):
    n = pl.program_id(0)
    channels = rows_ref.shape[1]
    count = centre.shape[0]
    gamma = count * count / 1152.0

    @pl.when(n == 0)
    def _():
        w_out_t[...] = jnp.broadcast_to(w_out_ref[...], (channels, LANES)).T
        centre[...] = centers(count)[0]
        grad_radial[...] = jnp.zeros_like(grad_radial)
        grad_source[...] = jnp.zeros_like(grad_source)
        grad_out[...] = jnp.zeros_like(grad_out)

    lane = index_ref[0, :PAD]
    row_of = index_ref[0, PAD:]
    source_back = pick_three(back_ref, 28, lane, row_of)
    lam = jnp.zeros((PAD, LANES), F32)
    for c in range(3):
        lam = lam + (back_ref[pl.ds(PAD + 8 * c + n, 1), :] - source_back[c]) * scalar_ref[
            0, c * PAD : (c + 1) * PAD
        ]
    lam_ref[...] = 0.2 * lam
    first, second = node_terms(agg_ref[0])
    w_out = w_out_t[...]
    readout = first * w_out

    def gather(j, total):
        place = pl.ds(pl.multiple_of(j * LANES, LANES), LANES)
        return total + lam_ref[pl.ds(j, 1), :] * (
            query_ref[0, :, place].astype(F32) * slope_ref[0, :, place].astype(F32)
        )

    dread = lax.fori_loop(0, DEG, gather, jnp.zeros((channels, LANES), F32))
    grad_out[...] += dread * first
    plain = 0.2 * dread * w_out * second

    def piece(j, unused):
        place = pl.ds(pl.multiple_of(j * LANES, LANES), LANES)
        later = pl.ds(pl.multiple_of((DEG + j) * LANES, LANES), LANES)
        bump, slant = basis(scalar_ref[0, pl.ds(3 * PAD + j, 1), :], centre[...], gamma)
        bases[:, place] = bump
        bases[:, later] = slant
        over_slope = lam_ref[pl.ds(j, 1), :] * readout
        query = query_ref[0, :, place].astype(F32)
        coefs[:, place] = (plain * query).astype(BF16)
        coefs[:, later] = (over_slope * query).astype(BF16)
        wants[:, place] = (
            over_slope * slope_ref[0, :, place].astype(F32)
            + plain * radial_ref[0, :, place].astype(F32)
        ).astype(BF16)
        return unused

    lax.fori_loop(0, DEG, piece, 0)
    grad_radial[...] += lax.dot_general(coefs[...], bases[...], NT, preferred_element_type=F32)
    grad_source[...] += lax.dot_general(rows_ref[0], wants[...], NT, preferred_element_type=F32)

    @pl.when(n == 6)
    def _():
        radial = grad_radial[...].T
        source = grad_source[...]
        out = jnp.sum(grad_out[...].T, axis=0, keepdims=True)
        for i in range(16):
            for k in range(3):
                at = (3 * i + k) * 8
                grads_ref[i, 8 * k : 8 * k + 8] = (
                    radial[at : at + 8] if at < count else source[at - count : at - count + 8]
                )
            grads_ref[i, 24:] = jnp.zeros((8, LANES), F32)
        grads_ref[0, 24:25] = out


def sum_kernel(
    groups,
    batches,
    grads_ref,
    loss_ref,
    radial_ref,
    source_ref,
    out_ref,
    total_loss_ref,
    first,
    part,
    whole,
    own,
    send_sem,
    recv_sem,
    dp_send,
    dp_recv,
    back_send,
    back_recv,
):
    me = lax.axis_index("graph")
    batch = lax.axis_index("dp")
    peers = [lax.rem(me + d, groups) for d in range(1, groups)]
    others = [lax.rem(batch + d, batches) for d in range(1, batches)]
    own[...] = grads_ref[...]
    own[0, 25:26] = loss_ref[0:1, :]
    greet([{"graph": p} for p in peers] + [{"dp": b} for b in others])
    copies = []
    for i, p in enumerate(peers):
        copies.append(send(own.at[p], first.at[i], send_sem.at[i], recv_sem.at[i], {"graph": p}))
    for copy in copies:
        copy.wait()
    total = own[me]
    for i in range(groups - 1):
        total = total + first[i]
    part[batch] = total
    copies = []
    for i, b in enumerate(others):
        copies.append(send(part.at[batch], part.at[batch], dp_send.at[i], dp_recv.at[i], {"dp": b}))
    for copy in copies:
        copy.wait()
    total = part[0]
    for i in range(1, batches):
        total = total + part[i]
    whole[me] = total
    copies = []
    for i, p in enumerate(peers):
        copies.append(send(whole.at[me], whole.at[me], back_send.at[i], back_recv.at[i], {"graph": p}))
    for copy in copies:
        copy.wait()
    count = radial_ref.shape[0]
    for i in range(groups):
        for k in range(3):
            at = (3 * i + k) * 8
            if at < count:
                radial_ref[at : at + 8] = whole[i, 8 * k : 8 * k + 8]
            else:
                source_ref[at - count : at - count + 8] = whole[i, 8 * k : 8 * k + 8]
    out_ref[...] = whole[0, 24:25]
    total_loss_ref[...] = whole[0, 25:26]


def whole_vmem():
    return pl.BlockSpec(memory_space=VMEM)


def local(
    node_state,
    atom_types,
    positions,
    force_ref,
    edge_source,
    edge_count,
    type_table,
    w_rad,
    w_src,
    w_out,
):
    nodes, channels = node_state.shape[1:]
    groups = lax.axis_size("graph")
    batches = lax.axis_size("dp")
    weight_loss = 1.0 / math.sqrt(3.0 * nodes * groups * node_state.shape[0] * batches)
    count = w_rad.shape[0]
    tiles = nodes // LANES
    wide = DEG * LANES
    dma = pltpu.SemaphoreType.DMA
    any_space = pl.BlockSpec(memory_space=pl.ANY)

    def shape(*dims, dtype=F32):
        return jax.ShapeDtypeStruct(dims, dtype)

    state, place = pl.pallas_call(
        functools.partial(halo_kernel, groups),
        out_shape=(shape(4, channels, nodes, dtype=BF16), shape(4, PAD, LANES)),
        in_specs=[whole_vmem()] * 4,
        out_specs=(any_space, any_space),
        scratch_shapes=[
            VMEM((channels, nodes), BF16),
            VMEM((PAD, LANES), F32),
            dma((6,)),
            dma((6,)),
            dma((2,)),
        ],
        compiler_params=pltpu.CompilerParams(collective_id=0, has_side_effects=True),
        name="halo",
    )(node_state[0], atom_types, positions[0], type_table)

    tile = lambda *dims: pl.BlockSpec((1,) + dims, lambda n: (n,) + (0,) * len(dims))
    fixed = lambda *dims: pl.BlockSpec(dims, lambda n: (0,) * len(dims))
    rows, query, slope, radial, scalar, index, agg, incoming, outgoing = pl.pallas_call(
        functools.partial(forward_kernel, groups),
        grid=(tiles,),
        out_shape=(
            *[shape(tiles, channels, wide, dtype=BF16)] * 4,
            shape(tiles, 4 * PAD, LANES),
            shape(tiles, 2 * PAD, LANES, dtype=jnp.int32),
            shape(tiles, channels, LANES),
            shape(PAD, LANES),
            shape(4 * PAD, LANES),
        ),
        in_specs=[
            fixed(4, channels, nodes),
            fixed(4 * PAD, LANES),
            fixed(DEG * tiles, LANES),
            pl.BlockSpec(memory_space=pltpu.SMEM),
            fixed(count, channels),
            fixed(channels, channels),
            fixed(1, channels),
        ],
        out_specs=(
            *[tile(channels, wide)] * 4,
            tile(4 * PAD, LANES),
            tile(2 * PAD, LANES),
            tile(channels, LANES),
            fixed(PAD, LANES),
            fixed(4 * PAD, LANES),
        ),
        scratch_shapes=[
            VMEM((14 * channels, 256), BF16),
            VMEM((channels, count), BF16),
            VMEM((channels, channels), BF16),
            VMEM((channels, LANES), F32),
            VMEM((count, LANES), F32),
            VMEM((3 * PAD, LANES), F32),
            VMEM((256, wide), BF16),
            VMEM((channels, wide), F32),
            VMEM((channels, LANES), F32),
            VMEM((96, 256), F32),
        ],
        compiler_params=pltpu.CompilerParams(vmem_limit_bytes=LIMIT),
        name="forward",
    )(
        state,
        place.reshape(4 * PAD, LANES),
        edge_source.reshape(DEG * tiles, LANES),
        edge_count,
        w_rad,
        w_src,
        w_out.reshape(1, channels),
    )

    forces, back, loss = pl.pallas_call(
        functools.partial(force_kernel, groups, weight_loss),
        out_shape=(shape(3, nodes), shape(4 * PAD, LANES), shape(8, LANES)),
        in_specs=[whole_vmem()] * 3,
        out_specs=(whole_vmem(),) * 3,
        scratch_shapes=[
            VMEM((3, PAD, LANES), F32),
            VMEM((PAD, LANES), F32),
            VMEM((PAD, LANES), F32),
            VMEM((3, PAD, LANES), F32),
            dma((6,)),
            dma((6,)),
        ],
        compiler_params=pltpu.CompilerParams(collective_id=1, has_side_effects=True),
        name="force",
    )(outgoing, incoming, force_ref[0])

    grads = pl.pallas_call(
        backward_kernel,
        grid=(tiles,),
        out_shape=shape(16, 32, LANES),
        in_specs=[
            fixed(4 * PAD, LANES),
            tile(4 * PAD, LANES),
            tile(2 * PAD, LANES),
            tile(channels, LANES),
            *[tile(channels, wide)] * 4,
            fixed(1, channels),
        ],
        out_specs=fixed(16, 32, LANES),
        scratch_shapes=[
            VMEM((channels, LANES), F32),
            VMEM((count, LANES), F32),
            VMEM((PAD, LANES), F32),
            VMEM((channels, 2 * wide), BF16),
            VMEM((count, 2 * wide), BF16),
            VMEM((channels, wide), BF16),
            VMEM((channels, count), F32),
            VMEM((channels, channels), F32),
            VMEM((channels, LANES), F32),
        ],
        compiler_params=pltpu.CompilerParams(vmem_limit_bytes=LIMIT),
        name="backward",
    )(back, scalar, index, agg, rows, query, slope, radial, w_out.reshape(1, channels))

    grad_radial, grad_source, grad_out, total_loss = pl.pallas_call(
        functools.partial(sum_kernel, groups, batches),
        out_shape=(
            shape(count, channels),
            shape(channels, channels),
            shape(1, channels),
            shape(1, LANES),
        ),
        in_specs=[whole_vmem()] * 2,
        out_specs=(whole_vmem(),) * 4,
        scratch_shapes=[
            VMEM((groups - 1, 32, LANES), F32),
            VMEM((batches, 32, LANES), F32),
            VMEM((groups, 32, LANES), F32),
            VMEM((groups, 32, LANES), F32),
            dma((groups - 1,)),
            dma((groups - 1,)),
            dma((max(batches - 1, 1),)),
            dma((max(batches - 1, 1),)),
            dma((groups - 1,)),
            dma((groups - 1,)),
        ],
        compiler_params=pltpu.CompilerParams(collective_id=2, has_side_effects=True),
        name="total",
    )(grads, loss)
    return forces[None], grad_radial, grad_source, grad_out[0], total_loss[0, 0]


def solution(mesh):
    in_specs = (
        P("dp", "graph", None),
        P("dp", "graph"),
        P("dp", None, "graph"),
        P("dp", None, "graph"),
        P("dp", "graph"),
        P("dp", "graph"),
        P(),
        P(),
        P(),
        P(),
    )
    out_specs = (P("dp", None, "graph"), P(), P(), P(), P())
    return jax.shard_map(local, mesh=mesh, in_specs=in_specs, out_specs=out_specs, check_vma=False)
```

```python
import functools
import math

import jax
import jax.numpy as jnp
from jax import lax
from jax.experimental import pallas as pl
from jax.experimental.pallas import tpu as pltpu
from jax.sharding import PartitionSpec as P

MESH = pl.DeviceIdType.MESH
F32 = jnp.float32
BF16 = jnp.bfloat16
NT = (((1,), (1,)), ((), ()))
DEG = 20
PAD = 24
LANES = 128
VMEM = pltpu.VMEM
LIMIT = 60 * 1024 * 1024
STEP = 10
WIDE = STEP * LANES


def partners(groups):
    me = lax.axis_index("graph")
    left = lax.rem(me + groups - 1, groups)
    right = lax.rem(me + 1, groups)
    far = lax.rem(me + groups // 2, groups)
    return left, right, far


def greet(devices):
    barrier = pltpu.get_barrier_semaphore()
    for device in devices:
        pl.semaphore_signal(barrier, inc=1, device_id=device, device_id_type=MESH)
    pl.semaphore_wait(barrier, len(devices))


def send(src, dst, send_sem, recv_sem, device):
    copy = pltpu.make_async_remote_copy(
        src_ref=src,
        dst_ref=dst,
        send_sem=send_sem,
        recv_sem=recv_sem,
        device_id=device,
        device_id_type=MESH,
    )
    copy.start()
    return copy


def lane_pick(row, index):
    return jnp.take_along_axis(
        jnp.broadcast_to(row, index.shape), index, axis=1, mode="promise_in_bounds"
    )


def pick_three(tab_ref, rows, lane, row_of):
    result = [jnp.zeros(lane.shape, F32)] * 3
    for r in range(rows):
        here = row_of == r
        for c in range(3):
            at = c * 8 + r % 7
            result[c] = jnp.where(
                here, lane_pick(tab_ref[r // 7, at : at + 1, :], lane), result[c]
            )
    return result


def basis(dist_row, scaled_centers, gamma):
    diff = (-2.0 * gamma) * dist_row - scaled_centers
    bump = jnp.exp2(diff * diff * (-math.log2(math.e) / (4.0 * gamma)))
    return bump.astype(BF16), (diff * bump).astype(BF16)


def centers(count):
    gamma = count * count / 1152.0
    number = lax.broadcasted_iota(jnp.int32, (count, LANES), 0).astype(F32)
    return number * (12.0 / count) * (-2.0 * gamma), gamma


def node_terms(agg):
    sig = jax.nn.sigmoid(agg)
    first = sig * (1.0 + agg * (1.0 - sig))
    second = sig * (1.0 - sig) * (2.0 + agg * (1.0 - 2.0 * sig))
    return first, second


def prepare_indices(groups, source_ref, count_ref, lanes_ref, rows_ref, pick_ref, tiles):
    me = lax.axis_index("graph")
    slot = lax.broadcasted_iota(jnp.int32, (PAD, LANES), 1) * DEG + lax.broadcasted_iota(
        jnp.int32, (PAD, LANES), 0
    )
    lane = slot & (LANES - 1)
    row_of = slot >> 7
    nodes = tiles * LANES
    for n in range(tiles):
        source = jnp.zeros((PAD, LANES), jnp.int32)
        for r in range(DEG):
            at = (n * DEG + r) * LANES
            source = jnp.where(row_of == r, lane_pick(source_ref[:, at : at + LANES], lane), source)
        block = (source * 74899) >> 26
        offset = (block - me + groups) & (groups - 1)
        position = jnp.where(
            offset == groups - 1, 0, jnp.where(offset == 0, 1, jnp.where(offset == 1, 2, 3))
        )
        picked = position * nodes + source - block * nodes
        live = slot + n * (DEG * LANES) < count_ref[...]
        lanes_ref[n] = picked & (LANES - 1)
        rows_ref[n] = picked >> 7
        pick_ref[n, :PAD] = jnp.where(live, (picked & 255).astype(F32), -1.0)
        pick_ref[n, PAD:] = (picked >> 8).astype(F32)


def fused_kernel(
    groups,
    batches,
    weight_loss,
    state_ref,
    types_ref,
    place_ref,
    wanted_ref,
    source_ref,
    count_ref,
    table_ref,
    w_rad_ref,
    w_src_ref,
    w_out_ref,
    forces_ref,
    whole_ref,
    states,
    places,
    stack,
    w_rad_t,
    w_src_t,
    w_out_t,
    centre,
    lanes,
    rows_of,
    pick,
    scalar,
    bumps,
    slants,
    rows_keep,
    query_keep,
    slope_keep,
    radial_keep,
    agg_keep,
    onehots,
    product,
    agg_acc,
    spread,
    incoming,
    outgoing,
    terms,
    wanted,
    backs,
    lam_ref,
    plain_coef,
    slope_coef,
    wants,
    grad_radial,
    grad_source,
    grad_out,
    own,
    pieces,
    part,
    whole,
    halo_send,
    halo_recv,
    term_send,
    term_recv,
    piece_send,
    piece_recv,
    part_send,
    part_recv,
    whole_send,
    whole_recv,
):
    nodes, channels = state_ref.shape
    tiles = nodes // LANES
    kinds = table_ref.shape[0]
    count = w_rad_ref.shape[0]
    gamma = count * count / 1152.0
    me = lax.axis_index("graph")
    batch = lax.axis_index("dp")
    left, right, far = partners(groups)
    near_by = (left, right, far)
    peers = [lax.rem(me + d, groups) for d in range(1, groups)]
    others = [lax.rem(batch + d, batches) for d in range(1, batches)]

    barrier = pltpu.get_barrier_semaphore()
    for device in [{"graph": p} for p in peers] + [{"dp": b} for b in others]:
        pl.semaphore_signal(barrier, inc=1, device_id=device, device_id_type=MESH)

    places[1] = jnp.zeros((PAD, LANES), F32)
    wanted[...] = jnp.zeros_like(wanted)
    for c in range(3):
        for n in range(tiles):
            at = slice(n * LANES, (n + 1) * LANES)
            places[1, 8 * c + n : 8 * c + n + 1, :] = place_ref[c, :, at]
            wanted[8 * c + n : 8 * c + n + 1, :] = wanted_ref[c, :, at]
    kind = (types_ref[...] == lax.broadcasted_iota(jnp.int32, (kinds, nodes), 0)).astype(BF16)
    embedded = lax.dot_general(
        table_ref[...], kind, (((0,), (0,)), ((), ())), preferred_element_type=F32
    )
    states[1] = (state_ref[...].astype(F32).T + embedded).astype(BF16)
    pl.semaphore_wait(barrier, len(peers) + len(others))
    place_copies, state_copies = [], []
    for i, (device, slot) in enumerate(((left, 2), (right, 0), (far, 3))):
        place_copies.append(
            send(places.at[1], places.at[slot], halo_send.at[i], halo_recv.at[i], {"graph": device})
        )
    for i, (device, slot) in enumerate(((left, 2), (right, 0), (far, 3))):
        state_copies.append(
            send(
                states.at[1], states.at[slot], halo_send.at[3 + i], halo_recv.at[3 + i], {"graph": device}
            )
        )

    w_rad_t[...] = w_rad_ref[...].astype(F32).T.astype(BF16)
    w_src_t[...] = w_src_ref[...].astype(F32).T.astype(BF16)
    w_out_t[...] = jnp.broadcast_to(w_out_ref[...], (channels, LANES)).T
    centre[...] = centers(count)[0]
    spread[...] = jnp.zeros_like(spread)
    incoming[...] = jnp.zeros_like(incoming)
    grad_radial[...] = jnp.zeros_like(grad_radial)
    grad_source[...] = jnp.zeros_like(grad_source)
    grad_out[...] = jnp.zeros_like(grad_out)
    prepare_indices(groups, source_ref, count_ref, lanes, rows_of, pick, tiles)
    for copy in place_copies:
        copy.wait()

    def distances(n, table_rows):
        source_place = pick_three(places, table_rows, lanes[n], rows_of[n])
        delta = [source_place[c] - places[1, pl.ds(8 * c + n, 1), :] for c in range(3)]
        dist = jnp.sqrt(delta[0] * delta[0] + delta[1] * delta[1] + delta[2] * delta[2] + 0.25)
        for c in range(3):
            scalar[n, c * PAD : (c + 1) * PAD] = delta[c] / dist
        scalar[n, 3 * PAD :] = dist

    def bases(n):
        def one(j, unused):
            place = pl.ds(pl.multiple_of(j * LANES, LANES), LANES)
            bump, slant = basis(scalar[n, pl.ds(3 * PAD + j, 1), :], centre[...], gamma)
            bumps[n, :, place] = bump
            slants[n, :, place] = slant
            return unused

        lax.fori_loop(0, DEG, one, 0)

    def before(n, unused):
        distances(n, 21)
        bases(n)
        return unused

    lax.fori_loop(1, tiles, before, 0)
    distances(0, 28)
    bases(0)
    for copy in state_copies:
        copy.wait()
    for half in range(28):
        at = (half % 7) * LANES
        stack[
            (half // 2) * channels : (half // 2 + 1) * channels,
            (half % 2) * LANES : (half % 2 + 1) * LANES,
        ] = states[half // 7, :, at : at + LANES]

    def forward(n, chunks):
        agg_acc[...] = jnp.zeros_like(agg_acc)

        def piece(i, unused):
            place = pl.ds(pl.multiple_of(i * WIDE, WIDE), WIDE)
            numbers = lax.broadcasted_iota(jnp.int32, (256, LANES), 0).astype(F32)
            ones, hi = [], []
            for j in range(STEP):
                column = pick[n, pl.ds(i * STEP + j, 1), :]
                ones.append((numbers == column).astype(BF16))
                hi.append(pick[n, pl.ds(PAD + i * STEP + j, 1), :])
            ones = jnp.concatenate(ones, axis=1)
            hi = jnp.broadcast_to(jnp.concatenate(hi, axis=1), (channels, WIDE))
            onehots[:, place] = ones
            found = jnp.dot(stack[: chunks * channels], ones, preferred_element_type=F32)
            rows = found[:channels]
            for c in range(1, chunks):
                rows = jnp.where(hi == float(c), found[c * channels : (c + 1) * channels], rows)
            rows = rows.astype(BF16)
            rows_keep[n, :, place] = rows
            query = jnp.dot(w_src_t[...], rows, preferred_element_type=F32)
            radial = jnp.dot(w_rad_t[...], bumps[n, :, place], preferred_element_type=F32)
            slope = jnp.dot(w_rad_t[...], slants[n, :, place], preferred_element_type=F32)
            query_keep[n, :, place] = query.astype(BF16)
            slope_keep[n, :, place] = slope.astype(BF16)
            radial_keep[n, :, place] = radial.astype(BF16)
            product[:, place] = query * slope
            term = radial * query
            total = term[:, :LANES]
            for j in range(1, STEP):
                total = total + term[:, j * LANES : (j + 1) * LANES]
            agg_acc[...] += total
            return unused

        lax.fori_loop(0, DEG // STEP, piece, 0)
        agg = 0.2 * agg_acc[...]
        agg_keep[n] = agg
        first, _ = node_terms(agg)
        readout = 0.2 * first * w_out_t[...]
        inward = [jnp.zeros((1, LANES), F32)] * 3
        lhs = []
        chunk = lax.broadcasted_iota(jnp.int32, (16, LANES), 0).astype(F32)
        for j in range(DEG):
            pull = jnp.sum(readout * product[:, j * LANES : (j + 1) * LANES], axis=0, keepdims=True)
            here = chunk == pick[n, PAD + j : PAD + j + 1, :]
            high, low = [], []
            for c in range(3):
                moved = pull * scalar[n, c * PAD + j : c * PAD + j + 1, :]
                inward[c] = inward[c] + moved
                term = jnp.where(here, moved, 0.0)
                top = term.astype(BF16)
                high.append(top)
                low.append((term - top.astype(F32)).astype(BF16))
            lhs.append(jnp.concatenate(high + low, axis=0))
        lhs = jnp.concatenate(lhs, axis=1)
        spread[...] += lax.dot_general(lhs, onehots[...], NT, preferred_element_type=F32)
        for c in range(3):
            incoming[pl.ds(8 * c + n, 1), :] = inward[c]

    lax.fori_loop(1, tiles, lambda n, u: (forward(n, 11), u)[1], 0)
    forward(0, 14)

    outgoing[...] = jnp.zeros_like(outgoing)
    total = spread[:48] + spread[48:]
    for c in range(3):
        for r in range(28):
            at = c * 8 + r % 7
            outgoing[r // 7, at : at + 1, :] = total[
                c * 16 + r // 2 : c * 16 + r // 2 + 1, (r % 2) * LANES : (r % 2 + 1) * LANES
            ]
    copies = []
    for i, (device, slot) in enumerate(((left, 0), (right, 2), (far, 3))):
        copies.append(
            send(outgoing.at[slot], terms.at[i], term_send.at[i], term_recv.at[i], {"graph": device})
        )
    for copy in copies:
        copy.wait()
    forces = incoming[...] - (outgoing[1] + terms[0] + terms[1] + terms[2])
    miss = forces - wanted[...]
    backs[1] = 2.0 * weight_loss * miss
    copies = []
    for i, (device, slot) in enumerate(((left, 2), (right, 0), (far, 3))):
        copies.append(
            send(backs.at[1], backs.at[slot], term_send.at[3 + i], term_recv.at[3 + i], {"graph": device})
        )
    for c in range(3):
        for n in range(tiles):
            forces_ref[c, :, n * LANES : (n + 1) * LANES] = forces[8 * c + n : 8 * c + n + 1, :]
    loss = weight_loss * jnp.sum(miss * miss, axis=(0, 1), keepdims=True)
    for copy in copies:
        copy.wait()

    def backward(n, table_rows):
        source_back = pick_three(backs, table_rows, lanes[n], rows_of[n])
        lam = jnp.zeros((PAD, LANES), F32)
        for c in range(3):
            lam = lam + (backs[1, pl.ds(8 * c + n, 1), :] - source_back[c]) * scalar[
                n, c * PAD : (c + 1) * PAD
            ]
        lam_ref[...] = 0.2 * lam
        first, second = node_terms(agg_keep[n])
        w_out = w_out_t[...]
        readout = first * w_out

        def gather(j, total):
            place = pl.ds(pl.multiple_of(j * LANES, LANES), LANES)
            return total + lam_ref[pl.ds(j, 1), :] * (
                query_keep[n, :, place].astype(F32) * slope_keep[n, :, place].astype(F32)
            )

        dread = lax.fori_loop(0, DEG, gather, jnp.zeros((channels, LANES), F32))
        grad_out[...] += dread * first
        plain = 0.2 * dread * w_out * second

        def piece(j, unused):
            place = pl.ds(pl.multiple_of(j * LANES, LANES), LANES)
            over_slope = lam_ref[pl.ds(j, 1), :] * readout
            query = query_keep[n, :, place].astype(F32)
            plain_coef[:, place] = (plain * query).astype(BF16)
            slope_coef[:, place] = (over_slope * query).astype(BF16)
            wants[:, place] = (
                over_slope * slope_keep[n, :, place].astype(F32)
                + plain * radial_keep[n, :, place].astype(F32)
            ).astype(BF16)
            return unused

        lax.fori_loop(0, DEG, piece, 0)
        grad_radial[...] += lax.dot_general(
            plain_coef[...], bumps[n], NT, preferred_element_type=F32
        ) + lax.dot_general(slope_coef[...], slants[n], NT, preferred_element_type=F32)
        grad_source[...] += lax.dot_general(
            rows_keep[n], wants[...], NT, preferred_element_type=F32
        )

    lax.fori_loop(1, tiles, lambda n, u: (backward(n, 21), u)[1], 0)
    backward(0, 28)

    radial = grad_radial[...].T
    source = grad_source[...]
    for i in range(groups):
        for k in range(3):
            at = (3 * i + k) * 8
            own[i, 8 * k : 8 * k + 8] = (
                radial[at : at + 8] if at < count else source[at - count : at - count + 8]
            )
        own[i, 24:] = jnp.zeros((8, LANES), F32)
    own[0, 24:25] = jnp.sum(grad_out[...].T, axis=0, keepdims=True)
    own[0, 25:26] = jnp.broadcast_to(loss, (1, LANES))
    copies = []
    for i, p in enumerate(peers):
        copies.append(send(own.at[p], pieces.at[i], piece_send.at[i], piece_recv.at[i], {"graph": p}))
    for copy in copies:
        copy.wait()
    total = own[me]
    for i in range(groups - 1):
        total = total + pieces[i]
    part[batch] = total
    copies = []
    for i, b in enumerate(others):
        copies.append(send(part.at[batch], part.at[batch], part_send.at[i], part_recv.at[i], {"dp": b}))
    for copy in copies:
        copy.wait()
    total = part[0]
    for i in range(1, batches):
        total = total + part[i]
    whole[me] = total
    copies = []
    for i, p in enumerate(peers):
        copies.append(send(whole.at[me], whole.at[me], whole_send.at[i], whole_recv.at[i], {"graph": p}))
    for copy in copies:
        copy.wait()
    whole_ref[...] = whole[...]


def output_kernel(whole_ref, from_ref, forces_ref, radial_ref, source_ref, out_ref, loss_ref):
    count = radial_ref.shape[0]
    for i in range(whole_ref.shape[0]):
        for k in range(3):
            at = (3 * i + k) * 8
            if at < count:
                radial_ref[at : at + 8] = whole_ref[i, 8 * k : 8 * k + 8]
            else:
                source_ref[at - count : at - count + 8] = whole_ref[i, 8 * k : 8 * k + 8]
    out_ref[...] = whole_ref[0, 24:25]
    loss_ref[...] = whole_ref[0, 25:26, :1]
    forces_ref[...] = from_ref[...]


def whole_vmem():
    return pl.BlockSpec(memory_space=VMEM)


def local(
    node_state,
    atom_types,
    positions,
    force_ref,
    edge_source,
    edge_count,
    type_table,
    w_rad,
    w_src,
    w_out,
):
    nodes, channels = node_state.shape[1:]
    groups = lax.axis_size("graph")
    batches = lax.axis_size("dp")
    weight_loss = 1.0 / math.sqrt(3.0 * nodes * groups * node_state.shape[0] * batches)
    count = w_rad.shape[0]
    tiles = nodes // LANES
    wide = DEG * LANES
    dma = pltpu.SemaphoreType.DMA

    def shape(*dims, dtype=F32):
        return jax.ShapeDtypeStruct(dims, dtype)

    others = max(batches - 1, 1)
    forces, whole = pl.pallas_call(
        functools.partial(fused_kernel, groups, batches, weight_loss),
        out_shape=(shape(3, 1, nodes), shape(groups, 32, LANES)),
        in_specs=[whole_vmem()] * 10,
        out_specs=(whole_vmem(),) * 2,
        scratch_shapes=[
            VMEM((4, channels, nodes), BF16),
            VMEM((4, PAD, LANES), F32),
            VMEM((14 * channels, 256), BF16),
            VMEM((channels, count), BF16),
            VMEM((channels, channels), BF16),
            VMEM((channels, LANES), F32),
            VMEM((count, LANES), F32),
            VMEM((tiles, PAD, LANES), jnp.int32),
            VMEM((tiles, PAD, LANES), jnp.int32),
            VMEM((tiles, 2 * PAD, LANES), F32),
            VMEM((tiles, 4 * PAD, LANES), F32),
            VMEM((tiles, count, wide), BF16),
            VMEM((tiles, count, wide), BF16),
            VMEM((tiles, channels, wide), BF16),
            VMEM((tiles, channels, wide), BF16),
            VMEM((tiles, channels, wide), BF16),
            VMEM((tiles, channels, wide), BF16),
            VMEM((tiles, channels, LANES), F32),
            VMEM((256, wide), BF16),
            VMEM((channels, wide), F32),
            VMEM((channels, LANES), F32),
            VMEM((96, 256), F32),
            VMEM((PAD, LANES), F32),
            VMEM((4, PAD, LANES), F32),
            VMEM((3, PAD, LANES), F32),
            VMEM((PAD, LANES), F32),
            VMEM((4, PAD, LANES), F32),
            VMEM((PAD, LANES), F32),
            VMEM((channels, wide), BF16),
            VMEM((channels, wide), BF16),
            VMEM((channels, wide), BF16),
            VMEM((channels, count), F32),
            VMEM((channels, channels), F32),
            VMEM((channels, LANES), F32),
            VMEM((groups, 32, LANES), F32),
            VMEM((groups - 1, 32, LANES), F32),
            VMEM((batches, 32, LANES), F32),
            VMEM((groups, 32, LANES), F32),
            dma((6,)),
            dma((6,)),
            dma((6,)),
            dma((6,)),
            dma((groups - 1,)),
            dma((groups - 1,)),
            dma((others,)),
            dma((others,)),
            dma((groups - 1,)),
            dma((groups - 1,)),
        ],
        compiler_params=pltpu.CompilerParams(
            collective_id=0, has_side_effects=True, vmem_limit_bytes=LIMIT
        ),
        name="fused",
    )(
        node_state[0],
        atom_types,
        positions.transpose(1, 0, 2),
        force_ref.transpose(1, 0, 2),
        edge_source,
        edge_count,
        type_table,
        w_rad,
        w_src,
        w_out.reshape(1, channels),
    )
    forces, grad_radial, grad_source, grad_out, loss = pl.pallas_call(
        output_kernel,
        out_shape=(
            shape(3, 1, nodes),
            shape(count, channels),
            shape(channels, channels),
            shape(1, channels),
            shape(1, 1),
        ),
        in_specs=[whole_vmem()] * 2,
        out_specs=(whole_vmem(),) * 5,
        name="output",
    )(whole, forces)
    return forces.transpose(1, 0, 2), grad_radial, grad_source, grad_out[0], loss[0, 0]


def solution(mesh):
    in_specs = (
        P("dp", "graph", None),
        P("dp", "graph"),
        P("dp", None, "graph"),
        P("dp", None, "graph"),
        P("dp", "graph"),
        P("dp", "graph"),
        P(),
        P(),
        P(),
        P(),
    )
    out_specs = (P("dp", None, "graph"), P(), P(), P(), P())
    return jax.shard_map(local, mesh=mesh, in_specs=in_specs, out_specs=out_specs, check_vma=False)
```

```python
import functools
import math

import jax
import jax.numpy as jnp
from jax import lax
from jax.experimental import pallas as pl
from jax.experimental.pallas import tpu as pltpu
from jax.sharding import PartitionSpec as P

MESH = pl.DeviceIdType.MESH
F32 = jnp.float32
BF16 = jnp.bfloat16
NT = (((1,), (1,)), ((), ()))
DEG = 20
PAD = 24
LANES = 128
VMEM = pltpu.VMEM
LIMIT = 60 * 1024 * 1024
WIDE = DEG * LANES


def partners(groups):
    me = lax.axis_index("graph")
    left = lax.rem(me + groups - 1, groups)
    right = lax.rem(me + 1, groups)
    far = lax.rem(me + groups // 2, groups)
    return left, right, far


def greet(devices):
    barrier = pltpu.get_barrier_semaphore()
    for device in devices:
        pl.semaphore_signal(barrier, inc=1, device_id=device, device_id_type=MESH)
    pl.semaphore_wait(barrier, len(devices))


def send(src, dst, send_sem, recv_sem, device):
    copy = pltpu.make_async_remote_copy(
        src_ref=src,
        dst_ref=dst,
        send_sem=send_sem,
        recv_sem=recv_sem,
        device_id=device,
        device_id_type=MESH,
    )
    copy.start()
    return copy


def lane_pick(row, index):
    return jnp.take_along_axis(
        jnp.broadcast_to(row, index.shape), index, axis=1, mode="promise_in_bounds"
    )


def pick_three(tab_ref, rows, lane, row_of):
    result = [jnp.zeros(lane.shape, F32)] * 3
    for r in range(rows):
        here = row_of == r
        for c in range(3):
            at = c * 8 + r % 7
            result[c] = jnp.where(
                here, lane_pick(tab_ref[r // 7, at : at + 1, :], lane), result[c]
            )
    return result


def basis(dist_row, scaled_centers, gamma):
    diff = (-2.0 * gamma) * dist_row - scaled_centers
    bump = jnp.exp2(diff * diff * (-math.log2(math.e) / (4.0 * gamma)))
    return bump.astype(BF16), (diff * bump).astype(BF16)


def centers(count):
    gamma = count * count / 1152.0
    number = lax.broadcasted_iota(jnp.int32, (count, LANES), 0).astype(F32)
    return number * (12.0 / count) * (-2.0 * gamma), gamma


def node_terms(agg):
    sig = jax.nn.sigmoid(agg)
    first = sig * (1.0 + agg * (1.0 - sig))
    second = sig * (1.0 - sig) * (2.0 + agg * (1.0 - 2.0 * sig))
    return first, second


def prepare_indices(groups, source_ref, count_ref, lanes_ref, rows_ref, pick_ref, tiles):
    me = lax.axis_index("graph")
    slot = lax.broadcasted_iota(jnp.int32, (PAD, LANES), 1) * DEG + lax.broadcasted_iota(
        jnp.int32, (PAD, LANES), 0
    )
    lane = slot & (LANES - 1)
    row_of = slot >> 7
    nodes = tiles * LANES
    for n in range(tiles):
        source = jnp.zeros((PAD, LANES), jnp.int32)
        for r in range(DEG):
            at = (n * DEG + r) * LANES
            source = jnp.where(row_of == r, lane_pick(source_ref[:, at : at + LANES], lane), source)
        block = (source * 74899) >> 26
        offset = (block - me + groups) & (groups - 1)
        position = jnp.where(
            offset == groups - 1, 0, jnp.where(offset == 0, 1, jnp.where(offset == 1, 2, 3))
        )
        picked = position * nodes + source - block * nodes
        live = slot + n * (DEG * LANES) < count_ref[...]
        lanes_ref[n] = picked & (LANES - 1)
        rows_ref[n] = picked >> 7
        pick_ref[n, :PAD] = jnp.where(live, (picked & 255).astype(F32), -1.0)
        pick_ref[n, PAD:] = (picked >> 8).astype(F32)


def fused_kernel(
    groups,
    batches,
    weight_loss,
    state_ref,
    types_ref,
    place_ref,
    wanted_ref,
    source_ref,
    count_ref,
    table_ref,
    w_rad_ref,
    w_src_ref,
    w_out_ref,
    forces_ref,
    whole_ref,
    states,
    places,
    stack,
    w_rad_t,
    w_src_t,
    w_out_t,
    centre,
    lanes,
    rows_of,
    pick,
    scalar,
    bumps,
    slants,
    rows_keep,
    query_keep,
    slope_keep,
    radial_keep,
    agg_keep,
    onehots_a,
    onehots_b,
    product_a,
    product_b,
    spread,
    incoming,
    outgoing,
    terms,
    wanted,
    backs,
    plain_a,
    slope_a,
    wants_a,
    plain_b,
    slope_b,
    wants_b,
    grad_radial,
    grad_source,
    grad_out,
    own,
    pieces,
    part,
    whole,
    halo_send,
    halo_recv,
    term_send,
    term_recv,
    piece_send,
    piece_recv,
    part_send,
    part_recv,
    whole_send,
    whole_recv,
):
    nodes, channels = state_ref.shape
    tiles = nodes // LANES
    kinds = table_ref.shape[0]
    count = w_rad_ref.shape[0]
    gamma = count * count / 1152.0
    me = lax.axis_index("graph")
    batch = lax.axis_index("dp")
    left, right, far = partners(groups)
    near_by = (left, right, far)
    peers = [lax.rem(me + d, groups) for d in range(1, groups)]
    others = [lax.rem(batch + d, batches) for d in range(1, batches)]

    barrier = pltpu.get_barrier_semaphore()
    for device in [{"graph": p} for p in peers] + [{"dp": b} for b in others]:
        pl.semaphore_signal(barrier, inc=1, device_id=device, device_id_type=MESH)

    places[1] = jnp.zeros((PAD, LANES), F32)
    wanted[...] = jnp.zeros_like(wanted)
    for c in range(3):
        for n in range(tiles):
            at = slice(n * LANES, (n + 1) * LANES)
            places[1, 8 * c + n : 8 * c + n + 1, :] = place_ref[c, :, at]
            wanted[8 * c + n : 8 * c + n + 1, :] = wanted_ref[c, :, at]
    kind = (types_ref[...] == lax.broadcasted_iota(jnp.int32, (kinds, nodes), 0)).astype(BF16)
    embedded = lax.dot_general(
        table_ref[...], kind, (((0,), (0,)), ((), ())), preferred_element_type=F32
    )
    states[1] = (state_ref[...].astype(F32).T + embedded).astype(BF16)
    pl.semaphore_wait(barrier, len(peers) + len(others))
    place_copies, state_copies = [], []
    for i, (device, slot) in enumerate(((left, 2), (right, 0), (far, 3))):
        place_copies.append(
            send(places.at[1], places.at[slot], halo_send.at[i], halo_recv.at[i], {"graph": device})
        )
    for i, (device, slot) in enumerate(((left, 2), (right, 0), (far, 3))):
        state_copies.append(
            send(
                states.at[1], states.at[slot], halo_send.at[3 + i], halo_recv.at[3 + i], {"graph": device}
            )
        )

    w_rad_t[...] = w_rad_ref[...].astype(F32).T.astype(BF16)
    w_src_t[...] = w_src_ref[...].astype(F32).T.astype(BF16)
    w_out_t[...] = jnp.broadcast_to(w_out_ref[...], (channels, LANES)).T
    centre[...] = centers(count)[0]
    spread[...] = jnp.zeros_like(spread)
    incoming[...] = jnp.zeros_like(incoming)
    grad_radial[...] = jnp.zeros_like(grad_radial)
    grad_source[...] = jnp.zeros_like(grad_source)
    grad_out[...] = jnp.zeros_like(grad_out)
    prepare_indices(groups, source_ref, count_ref, lanes, rows_of, pick, tiles)
    for copy in place_copies:
        copy.wait()

    def distances(n, table_rows):
        source_place = pick_three(places, table_rows, lanes[n], rows_of[n])
        delta = [source_place[c] - places[1, pl.ds(8 * c + n, 1), :] for c in range(3)]
        dist = jnp.sqrt(delta[0] * delta[0] + delta[1] * delta[1] + delta[2] * delta[2] + 0.25)
        for c in range(3):
            scalar[n, c * PAD : (c + 1) * PAD] = delta[c] / dist
        scalar[n, 3 * PAD :] = dist

    def bases(n):
        def one(j, unused):
            place = pl.ds(pl.multiple_of(j * LANES, LANES), LANES)
            bump, slant = basis(scalar[n, pl.ds(3 * PAD + j, 1), :], centre[...], gamma)
            bumps[n, :, place] = bump
            slants[n, :, place] = slant
            return unused

        lax.fori_loop(0, DEG, one, 0)

    def before(n, unused):
        distances(n, 21)
        bases(n)
        return unused

    lax.fori_loop(1, tiles, before, 0)
    distances(0, 28)
    bases(0)
    for copy in state_copies:
        copy.wait()
    for half in range(28):
        at = (half % 7) * LANES
        stack[
            (half // 2) * channels : (half // 2 + 1) * channels,
            (half % 2) * LANES : (half % 2 + 1) * LANES,
        ] = states[half // 7, :, at : at + LANES]

    def gather(n, chunks, onehots, product):
        numbers = lax.broadcasted_iota(jnp.int32, (256, LANES), 0).astype(F32)
        ones = jnp.concatenate(
            [(numbers == pick[n, pl.ds(j, 1), :]).astype(BF16) for j in range(DEG)], axis=1
        )
        hi = jnp.concatenate([pick[n, pl.ds(PAD + j, 1), :] for j in range(DEG)], axis=1)
        hi = jnp.broadcast_to(hi, (channels, WIDE))
        found = jnp.dot(stack[: chunks * channels], ones, preferred_element_type=F32)
        onehots[...] = ones
        rows = found[:channels]
        for c in range(1, chunks):
            rows = jnp.where(hi == float(c), found[c * channels : (c + 1) * channels], rows)
        rows = rows.astype(BF16)
        rows_keep[n] = rows
        query = jnp.dot(w_src_t[...], rows, preferred_element_type=F32)
        radial = jnp.dot(w_rad_t[...], bumps[n], preferred_element_type=F32)
        slope = jnp.dot(w_rad_t[...], slants[n], preferred_element_type=F32)
        query_keep[n] = query.astype(BF16)
        slope_keep[n] = slope.astype(BF16)
        radial_keep[n] = radial.astype(BF16)
        product[...] = query * slope
        term = radial * query
        total = term[:, :LANES]
        for j in range(1, DEG):
            total = total + term[:, j * LANES : (j + 1) * LANES]
        agg_keep[n] = 0.2 * total

    def pull(n, onehots, product):
        first, _ = node_terms(agg_keep[n])
        readout = 0.2 * first * w_out_t[...]
        inward = [jnp.zeros((1, LANES), F32)] * 3
        lhs = []
        chunk = lax.broadcasted_iota(jnp.int32, (16, LANES), 0).astype(F32)
        for j in range(DEG):
            force = jnp.sum(readout * product[:, j * LANES : (j + 1) * LANES], axis=0, keepdims=True)
            here = chunk == pick[n, PAD + j : PAD + j + 1, :]
            high, low = [], []
            for c in range(3):
                moved = force * scalar[n, c * PAD + j : c * PAD + j + 1, :]
                inward[c] = inward[c] + moved
                term = jnp.where(here, moved, 0.0)
                top = term.astype(BF16)
                high.append(top)
                low.append((term - top.astype(F32)).astype(BF16))
            lhs.append(jnp.concatenate(high + low, axis=0))
        lhs = jnp.concatenate(lhs, axis=1)
        spread[...] += lax.dot_general(lhs, onehots[...], NT, preferred_element_type=F32)
        for c in range(3):
            incoming[pl.ds(8 * c + n, 1), :] = inward[c]

    agg_keep[0] = jnp.zeros((channels, LANES), F32)
    product_b[...] = jnp.zeros_like(product_b)
    onehots_b[...] = jnp.zeros_like(onehots_b)

    def two_forward(i, unused):
        n = 2 * i + 1
        pull(n - 1, onehots_b, product_b)
        gather(n, 11, onehots_a, product_a)
        pull(n, onehots_a, product_a)
        gather(n + 1, 11, onehots_b, product_b)
        return unused

    lax.fori_loop(0, (tiles - 1) // 2, two_forward, 0)
    pull(tiles - 1, onehots_b, product_b)
    gather(0, 14, onehots_a, product_a)
    pull(0, onehots_a, product_a)

    outgoing[...] = jnp.zeros_like(outgoing)
    total = spread[:48] + spread[48:]
    for c in range(3):
        for r in range(28):
            at = c * 8 + r % 7
            outgoing[r // 7, at : at + 1, :] = total[
                c * 16 + r // 2 : c * 16 + r // 2 + 1, (r % 2) * LANES : (r % 2 + 1) * LANES
            ]
    copies = []
    for i, (device, slot) in enumerate(((left, 0), (right, 2), (far, 3))):
        copies.append(
            send(outgoing.at[slot], terms.at[i], term_send.at[i], term_recv.at[i], {"graph": device})
        )
    for copy in copies:
        copy.wait()
    forces = incoming[...] - (outgoing[1] + terms[0] + terms[1] + terms[2])
    miss = forces - wanted[...]
    backs[1] = 2.0 * weight_loss * miss
    copies = []
    for i, (device, slot) in enumerate(((left, 2), (right, 0), (far, 3))):
        copies.append(
            send(backs.at[1], backs.at[slot], term_send.at[3 + i], term_recv.at[3 + i], {"graph": device})
        )
    for c in range(3):
        for n in range(tiles):
            forces_ref[c, :, n * LANES : (n + 1) * LANES] = forces[8 * c + n : 8 * c + n + 1, :]
    loss = weight_loss * jnp.sum(miss * miss, axis=(0, 1), keepdims=True)
    for copy in copies:
        copy.wait()

    def coefficients(n, table_rows, plain_coef, slope_coef, wants):
        source_back = pick_three(backs, table_rows, lanes[n], rows_of[n])
        lam = jnp.zeros((PAD, LANES), F32)
        for c in range(3):
            lam = lam + (backs[1, pl.ds(8 * c + n, 1), :] - source_back[c]) * scalar[
                n, c * PAD : (c + 1) * PAD
            ]
        lam = 0.2 * lam
        first, second = node_terms(agg_keep[n])
        w_out = w_out_t[...]
        readout = first * w_out
        dread = jnp.zeros((channels, LANES), F32)
        for j in range(DEG):
            at = slice(j * LANES, (j + 1) * LANES)
            dread = dread + lam[j : j + 1] * (
                query_keep[n, :, at].astype(F32) * slope_keep[n, :, at].astype(F32)
            )
        grad_out[...] += dread * first
        plain = 0.2 * dread * w_out * second
        for j in range(DEG):
            at = slice(j * LANES, (j + 1) * LANES)
            over_slope = lam[j : j + 1] * readout
            query = query_keep[n, :, at].astype(F32)
            plain_coef[:, at] = (plain * query).astype(BF16)
            slope_coef[:, at] = (over_slope * query).astype(BF16)
            wants[:, at] = (
                over_slope * slope_keep[n, :, at].astype(F32)
                + plain * radial_keep[n, :, at].astype(F32)
            ).astype(BF16)

    def products(n, plain_coef, slope_coef, wants):
        grad_radial[...] += lax.dot_general(
            plain_coef[...], bumps[n], NT, preferred_element_type=F32
        ) + lax.dot_general(slope_coef[...], slants[n], NT, preferred_element_type=F32)
        grad_source[...] += lax.dot_general(
            rows_keep[n], wants[...], NT, preferred_element_type=F32
        )

    coef_a = (plain_a, slope_a, wants_a)
    coef_b = (plain_b, slope_b, wants_b)
    for ref in coef_b:
        ref[...] = jnp.zeros_like(ref)

    def two_backward(i, unused):
        n = 2 * i + 1
        products(n - 1, *coef_b)
        coefficients(n, 21, *coef_a)
        products(n, *coef_a)
        coefficients(n + 1, 21, *coef_b)
        return unused

    lax.fori_loop(0, (tiles - 1) // 2, two_backward, 0)
    products(tiles - 1, *coef_b)
    coefficients(0, 28, *coef_a)
    products(0, *coef_a)

    radial = grad_radial[...].T
    source = grad_source[...]
    for i in range(groups):
        for k in range(3):
            at = (3 * i + k) * 8
            own[i, 8 * k : 8 * k + 8] = (
                radial[at : at + 8] if at < count else source[at - count : at - count + 8]
            )
        own[i, 24:] = jnp.zeros((8, LANES), F32)
    own[0, 24:25] = jnp.sum(grad_out[...].T, axis=0, keepdims=True)
    own[0, 25:26] = jnp.broadcast_to(loss, (1, LANES))
    copies = []
    for i, p in enumerate(peers):
        copies.append(send(own.at[p], pieces.at[i], piece_send.at[i], piece_recv.at[i], {"graph": p}))
    for copy in copies:
        copy.wait()
    total = own[me]
    for i in range(groups - 1):
        total = total + pieces[i]
    part[batch] = total
    copies = []
    for i, b in enumerate(others):
        copies.append(send(part.at[batch], part.at[batch], part_send.at[i], part_recv.at[i], {"dp": b}))
    for copy in copies:
        copy.wait()
    total = part[0]
    for i in range(1, batches):
        total = total + part[i]
    whole[me] = total
    copies = []
    for i, p in enumerate(peers):
        copies.append(send(whole.at[me], whole.at[me], whole_send.at[i], whole_recv.at[i], {"graph": p}))
    for copy in copies:
        copy.wait()
    whole_ref[...] = whole[...]


def output_kernel(whole_ref, from_ref, forces_ref, radial_ref, source_ref, out_ref, loss_ref):
    count = radial_ref.shape[0]
    for i in range(whole_ref.shape[0]):
        for k in range(3):
            at = (3 * i + k) * 8
            if at < count:
                radial_ref[at : at + 8] = whole_ref[i, 8 * k : 8 * k + 8]
            else:
                source_ref[at - count : at - count + 8] = whole_ref[i, 8 * k : 8 * k + 8]
    out_ref[...] = whole_ref[0, 24:25]
    loss_ref[...] = whole_ref[0, 25:26, :1]
    forces_ref[...] = from_ref[...]


def whole_vmem():
    return pl.BlockSpec(memory_space=VMEM)


def local(
    node_state,
    atom_types,
    positions,
    force_ref,
    edge_source,
    edge_count,
    type_table,
    w_rad,
    w_src,
    w_out,
):
    nodes, channels = node_state.shape[1:]
    groups = lax.axis_size("graph")
    batches = lax.axis_size("dp")
    weight_loss = 1.0 / math.sqrt(3.0 * nodes * groups * node_state.shape[0] * batches)
    count = w_rad.shape[0]
    tiles = nodes // LANES
    wide = DEG * LANES
    dma = pltpu.SemaphoreType.DMA

    def shape(*dims, dtype=F32):
        return jax.ShapeDtypeStruct(dims, dtype)

    others = max(batches - 1, 1)
    forces, whole = pl.pallas_call(
        functools.partial(fused_kernel, groups, batches, weight_loss),
        out_shape=(shape(3, 1, nodes), shape(groups, 32, LANES)),
        in_specs=[whole_vmem()] * 10,
        out_specs=(whole_vmem(),) * 2,
        scratch_shapes=[
            VMEM((4, channels, nodes), BF16),
            VMEM((4, PAD, LANES), F32),
            VMEM((14 * channels, 256), BF16),
            VMEM((channels, count), BF16),
            VMEM((channels, channels), BF16),
            VMEM((channels, LANES), F32),
            VMEM((count, LANES), F32),
            VMEM((tiles, PAD, LANES), jnp.int32),
            VMEM((tiles, PAD, LANES), jnp.int32),
            VMEM((tiles, 2 * PAD, LANES), F32),
            VMEM((tiles, 4 * PAD, LANES), F32),
            VMEM((tiles, count, wide), BF16),
            VMEM((tiles, count, wide), BF16),
            VMEM((tiles, channels, wide), BF16),
            VMEM((tiles, channels, wide), BF16),
            VMEM((tiles, channels, wide), BF16),
            VMEM((tiles, channels, wide), BF16),
            VMEM((tiles, channels, LANES), F32),
            *[VMEM((256, wide), BF16)] * 2,
            *[VMEM((channels, wide), F32)] * 2,
            VMEM((96, 256), F32),
            VMEM((PAD, LANES), F32),
            VMEM((4, PAD, LANES), F32),
            VMEM((3, PAD, LANES), F32),
            VMEM((PAD, LANES), F32),
            VMEM((4, PAD, LANES), F32),
            *[VMEM((channels, wide), BF16)] * 6,
            VMEM((channels, count), F32),
            VMEM((channels, channels), F32),
            VMEM((channels, LANES), F32),
            VMEM((groups, 32, LANES), F32),
            VMEM((groups - 1, 32, LANES), F32),
            VMEM((batches, 32, LANES), F32),
            VMEM((groups, 32, LANES), F32),
            dma((6,)),
            dma((6,)),
            dma((6,)),
            dma((6,)),
            dma((groups - 1,)),
            dma((groups - 1,)),
            dma((others,)),
            dma((others,)),
            dma((groups - 1,)),
            dma((groups - 1,)),
        ],
        compiler_params=pltpu.CompilerParams(
            collective_id=0, has_side_effects=True, vmem_limit_bytes=LIMIT
        ),
        name="fused",
    )(
        node_state[0],
        atom_types,
        positions.transpose(1, 0, 2),
        force_ref.transpose(1, 0, 2),
        edge_source,
        edge_count,
        type_table,
        w_rad,
        w_src,
        w_out.reshape(1, channels),
    )
    forces, grad_radial, grad_source, grad_out, loss = pl.pallas_call(
        output_kernel,
        out_shape=(
            shape(3, 1, nodes),
            shape(count, channels),
            shape(channels, channels),
            shape(1, channels),
            shape(1, 1),
        ),
        in_specs=[whole_vmem()] * 2,
        out_specs=(whole_vmem(),) * 5,
        name="output",
    )(whole, forces)
    return forces.transpose(1, 0, 2), grad_radial, grad_source, grad_out[0], loss[0, 0]


def solution(mesh):
    in_specs = (
        P("dp", "graph", None),
        P("dp", "graph"),
        P("dp", None, "graph"),
        P("dp", None, "graph"),
        P("dp", "graph"),
        P("dp", "graph"),
        P(),
        P(),
        P(),
        P(),
    )
    out_specs = (P("dp", None, "graph"), P(), P(), P(), P())
    return jax.shard_map(local, mesh=mesh, in_specs=in_specs, out_specs=out_specs, check_vma=False)
```

```python
import functools
import math

import jax
import jax.numpy as jnp
from jax import lax
from jax.experimental import pallas as pl
from jax.experimental.pallas import tpu as pltpu
from jax.sharding import PartitionSpec as P

MESH = pl.DeviceIdType.MESH
F32 = jnp.float32
BF16 = jnp.bfloat16
NT = (((1,), (1,)), ((), ()))
DEG = 20
PAD = 24
LANES = 128
VMEM = pltpu.VMEM
LIMIT = 62 * 1024 * 1024
WIDE = DEG * LANES
NEAR = 16


def partners(groups):
    me = lax.axis_index("graph")
    left = lax.rem(me + groups - 1, groups)
    right = lax.rem(me + 1, groups)
    far = lax.rem(me + groups // 2, groups)
    return left, right, far


def greet(devices):
    barrier = pltpu.get_barrier_semaphore()
    for device in devices:
        pl.semaphore_signal(barrier, inc=1, device_id=device, device_id_type=MESH)
    pl.semaphore_wait(barrier, len(devices))


def send(src, dst, send_sem, recv_sem, device):
    copy = pltpu.make_async_remote_copy(
        src_ref=src,
        dst_ref=dst,
        send_sem=send_sem,
        recv_sem=recv_sem,
        device_id=device,
        device_id_type=MESH,
    )
    copy.start()
    return copy


def lane_pick(row, index):
    return jnp.take_along_axis(
        jnp.broadcast_to(row, index.shape), index, axis=1, mode="promise_in_bounds"
    )


def pick_three(tab_ref, rows, lane, row_of):
    result = [jnp.zeros(lane.shape, F32)] * 3
    for r in range(rows):
        here = row_of == r
        for c in range(3):
            at = c * 8 + r % 7
            result[c] = jnp.where(
                here, lane_pick(tab_ref[r // 7, at : at + 1, :], lane), result[c]
            )
    return result


def basis(dist_row, scaled_centers, gamma):
    diff = (-2.0 * gamma) * dist_row - scaled_centers
    bump = jnp.exp2(diff * diff * (-math.log2(math.e) / (4.0 * gamma)))
    return bump.astype(BF16), (diff * bump).astype(BF16)


def centers(count):
    gamma = count * count / 1152.0
    number = lax.broadcasted_iota(jnp.int32, (count, LANES), 0).astype(F32)
    return number * (12.0 / count) * (-2.0 * gamma), gamma


def node_terms(agg):
    sig = jax.nn.sigmoid(agg)
    first = sig * (1.0 + agg * (1.0 - sig))
    second = sig * (1.0 - sig) * (2.0 + agg * (1.0 - 2.0 * sig))
    return first, second


def prepare_indices(
    groups, source_ref, count_ref, lanes_ref, rows_ref, pick_ref, compact_ref, tiles
):
    me = lax.axis_index("graph")
    slot = lax.broadcasted_iota(jnp.int32, (PAD, LANES), 1) * DEG + lax.broadcasted_iota(
        jnp.int32, (PAD, LANES), 0
    )
    lane = slot & (LANES - 1)
    row_of = slot >> 7
    nodes = tiles * LANES
    for n in range(tiles):
        source = jnp.zeros((PAD, LANES), jnp.int32)
        for r in range(DEG):
            at = (n * DEG + r) * LANES
            source = jnp.where(row_of == r, lane_pick(source_ref[:, at : at + LANES], lane), source)
        block = (source * 74899) >> 26
        offset = (block - me + groups) & (groups - 1)
        position = jnp.where(
            offset == groups - 1, 0, jnp.where(offset == 0, 1, jnp.where(offset == 1, 2, 3))
        )
        picked = position * nodes + source - block * nodes
        live = slot + n * (DEG * LANES) < count_ref[...]
        lanes_ref[n] = picked & (LANES - 1)
        rows_ref[n] = picked >> 7
        pick_ref[n, :PAD] = jnp.where(live, (picked & 255).astype(F32), -1.0)
        pick_ref[n, PAD:] = (picked >> 8).astype(F32)
    lane = lax.broadcasted_iota(jnp.int32, (8, LANES), 1)
    here = (lane >> 4) == lax.broadcasted_iota(jnp.int32, (8, LANES), 0)
    for g in range(2):
        for r in range(PAD // 8):
            values = pick_ref[0, g * PAD + 8 * r : g * PAD + 8 * r + 8]
            values = jnp.take_along_axis(
                values, LANES - NEAR + (lane & (NEAR - 1)), axis=1, mode="promise_in_bounds"
            )
            compact_ref[8 * g + r : 8 * g + r + 1] = jnp.sum(
                jnp.where(here, values, 0.0), axis=0, keepdims=True
            )


def fused_kernel(
    groups,
    batches,
    weight_loss,
    state_ref,
    types_ref,
    place_ref,
    wanted_ref,
    source_ref,
    count_ref,
    table_ref,
    w_rad_ref,
    w_src_ref,
    w_out_ref,
    forces_ref,
    whole_ref,
    states,
    places,
    stack,
    w_rad_t,
    w_src_t,
    w_out_t,
    centre,
    lanes,
    rows_of,
    pick,
    compact,
    scalar,
    basis_a,
    basis_b,
    rows_keep,
    query_keep,
    slope_keep,
    radial_keep,
    agg_keep,
    onehots_a,
    onehots_b,
    product_a,
    product_b,
    spread,
    incoming,
    outgoing,
    terms,
    wanted,
    backs,
    wants_a,
    wants_b,
    grad_radial,
    grad_source,
    grad_out,
    own,
    pieces,
    part,
    whole,
    halo_send,
    halo_recv,
    term_send,
    term_recv,
    piece_send,
    piece_recv,
    part_send,
    part_recv,
    whole_send,
    whole_recv,
):
    nodes, channels = state_ref.shape
    tiles = nodes // LANES
    kinds = table_ref.shape[0]
    count = w_rad_ref.shape[0]
    gamma = count * count / 1152.0
    me = lax.axis_index("graph")
    batch = lax.axis_index("dp")
    left, right, far = partners(groups)
    near_by = (left, right, far)
    peers = [lax.rem(me + d, groups) for d in range(1, groups)]
    others = [lax.rem(batch + d, batches) for d in range(1, batches)]

    barrier = pltpu.get_barrier_semaphore()
    for device in [{"graph": p} for p in peers] + [{"dp": b} for b in others]:
        pl.semaphore_signal(barrier, inc=1, device_id=device, device_id_type=MESH)

    places[1] = jnp.zeros((PAD, LANES), F32)
    wanted[...] = jnp.zeros_like(wanted)
    for c in range(3):
        for n in range(tiles):
            at = slice(n * LANES, (n + 1) * LANES)
            places[1, 8 * c + n : 8 * c + n + 1, :] = place_ref[c, :, at]
            wanted[8 * c + n : 8 * c + n + 1, :] = wanted_ref[c, :, at]
    kind = (types_ref[...] == lax.broadcasted_iota(jnp.int32, (kinds, nodes), 0)).astype(BF16)
    embedded = lax.dot_general(
        table_ref[...], kind, (((0,), (0,)), ((), ())), preferred_element_type=F32
    )
    states[1] = (state_ref[...].astype(F32).T + embedded).astype(BF16)
    prepare_indices(groups, source_ref, count_ref, lanes, rows_of, pick, compact, tiles)
    pl.semaphore_wait(barrier, len(peers) + len(others))
    place_copies, state_copies = [], []
    targets = ((left, 2), (right, 0), (far, 3))
    for i, (device, slot) in enumerate(targets):
        place_copies.append(
            send(places.at[1], places.at[slot], halo_send.at[i], halo_recv.at[i], {"graph": device})
        )
    for i, (device, slot) in enumerate(targets):
        state_copies.append(
            send(
                states.at[1], states.at[slot], halo_send.at[3 + i], halo_recv.at[3 + i], {"graph": device}
            )
        )

    w_rad_t[...] = w_rad_ref[...].astype(F32).T.astype(BF16)
    w_src_t[...] = w_src_ref[...].astype(F32).T.astype(BF16)
    w_out_t[...] = jnp.broadcast_to(w_out_ref[...], (channels, LANES)).T
    centre[...] = centers(count)[0]
    spread[...] = jnp.zeros_like(spread)
    incoming[...] = jnp.zeros_like(incoming)
    grad_radial[...] = jnp.zeros_like(grad_radial)
    grad_source[...] = jnp.zeros_like(grad_source)
    grad_out[...] = jnp.zeros_like(grad_out)
    for copy in place_copies:
        copy.wait()

    def distances(n, table_rows):
        source_place = pick_three(places, table_rows, lanes[n], rows_of[n])
        delta = [source_place[c] - places[1, pl.ds(8 * c + n, 1), :] for c in range(3)]
        dist = jnp.sqrt(delta[0] * delta[0] + delta[1] * delta[1] + delta[2] * delta[2] + 0.25)
        for c in range(3):
            scalar[n, c * PAD : (c + 1) * PAD] = delta[c] / dist
        scalar[n, 3 * PAD :] = dist

    def bases(n, kept):
        for j in range(DEG):
            at = slice(j * LANES, (j + 1) * LANES)
            bump, slant = basis(scalar[n, 3 * PAD + j : 3 * PAD + j + 1, :], centre[...], gamma)
            kept[0, :, at] = bump
            kept[1, :, at] = slant

    def stack_up(halves):
        for half in halves:
            at = (half % 7) * LANES
            stack[
                (half // 2) * channels : (half // 2 + 1) * channels,
                (half % 2) * LANES : (half % 2 + 1) * LANES,
            ] = states[half // 7, :, at : at + LANES]

    lax.fori_loop(1, tiles, lambda n, u: (distances(n, 21), u)[1], 0)
    distances(0, 28)
    def ahead(i, u):
        bases(2 * i + 1, basis_a.at[i])
        bases(2 * i + 2, basis_b.at[i])
        return u

    lax.fori_loop(0, tiles // 2, ahead, 0)
    bases(0, basis_a.at[3])
    stack[10 * channels : 11 * channels, LANES:] = jnp.zeros((channels, LANES), BF16)
    for copy in state_copies[:2]:
        copy.wait()
    stack_up(range(21))

    numbers = lax.broadcasted_iota(jnp.int32, (256, LANES), 0).astype(F32)

    def look_up(columns, chosen, first, last):
        ones = jnp.concatenate([(numbers == column).astype(BF16) for column in columns], axis=1)
        hi = jnp.concatenate(chosen, axis=1)
        hi = jnp.broadcast_to(hi, (channels, hi.shape[1]))
        found = jnp.dot(
            stack[first * channels : last * channels], ones, preferred_element_type=F32
        )
        rows = found[:channels]
        for c in range(1, last - first):
            rows = jnp.where(
                hi == float(first + c), found[c * channels : (c + 1) * channels], rows
            )
        return ones, rows

    def gather(n, kept, onehots, product):
        columns = [pick[n, pl.ds(j, 1), :] for j in range(DEG)]
        chosen = [pick[n, pl.ds(PAD + j, 1), :] for j in range(DEG)]
        if isinstance(n, int):
            ones, rows = look_up(columns, chosen, 10, 14)
            _, near = look_up(
                [compact[r : r + 1] for r in range(3)], [compact[8 + r : 9 + r] for r in range(3)], 0, 11
            )
            last = lax.broadcasted_iota(jnp.int32, (channels, LANES), 1) >= LANES - NEAR
            parts = []
            for j in range(DEG):
                moved = pltpu.roll(
                    near[:, (j // 8) * LANES : (j // 8 + 1) * LANES],
                    LANES - NEAR - NEAR * (j % 8),
                    1,
                )
                parts.append(jnp.where(last, moved, rows[:, j * LANES : (j + 1) * LANES]))
            rows = jnp.concatenate(parts, axis=1)
        else:
            ones, rows = look_up(columns, chosen, 0, 11)
        onehots[...] = ones
        rows = rows.astype(BF16)
        rows_keep[n] = rows
        query = jnp.dot(w_src_t[...], rows, preferred_element_type=F32)
        radial = jnp.dot(w_rad_t[...], kept[0], preferred_element_type=F32)
        slope = jnp.dot(w_rad_t[...], kept[1], preferred_element_type=F32)
        query_keep[n] = query.astype(BF16)
        slope_keep[n] = slope.astype(BF16)
        radial_keep[n] = radial.astype(BF16)
        product[...] = query * slope
        term = radial * query
        total = term[:, :LANES]
        for j in range(1, DEG):
            total = total + term[:, j * LANES : (j + 1) * LANES]
        agg_keep[n] = 0.2 * total

    def pull(n, onehots, product):
        first, _ = node_terms(agg_keep[n])
        readout = 0.2 * first * w_out_t[...]
        inward = [jnp.zeros((1, LANES), F32)] * 3
        lhs = []
        chunk = lax.broadcasted_iota(jnp.int32, (16, LANES), 0).astype(F32)
        for j in range(DEG):
            force = jnp.sum(readout * product[:, j * LANES : (j + 1) * LANES], axis=0, keepdims=True)
            here = chunk == pick[n, PAD + j : PAD + j + 1, :]
            high, low = [], []
            for c in range(3):
                moved = force * scalar[n, c * PAD + j : c * PAD + j + 1, :]
                inward[c] = inward[c] + moved
                term = jnp.where(here, moved, 0.0)
                top = term.astype(BF16)
                high.append(top)
                low.append((term - top.astype(F32)).astype(BF16))
            lhs.append(jnp.concatenate(high + low, axis=0))
        lhs = jnp.concatenate(lhs, axis=1)
        spread[...] += lax.dot_general(lhs, onehots[...], NT, preferred_element_type=F32)
        for c in range(3):
            incoming[pl.ds(8 * c + n, 1), :] = inward[c]

    agg_keep[0] = jnp.zeros((channels, LANES), F32)
    product_b[...] = jnp.zeros_like(product_b)
    onehots_b[...] = jnp.zeros_like(onehots_b)

    def two_forward(i, unused):
        n = 2 * i + 1
        pull(n - 1, onehots_b, product_b)
        gather(n, basis_a.at[i], onehots_a, product_a)
        pull(n, onehots_a, product_a)
        gather(n + 1, basis_b.at[i], onehots_b, product_b)
        return unused

    lax.fori_loop(0, (tiles - 1) // 2, two_forward, 0)
    state_copies[2].wait()
    stack_up(range(21, 28))
    pull(tiles - 1, onehots_b, product_b)
    gather(0, basis_a.at[tiles // 2], onehots_a, product_a)
    pull(0, onehots_a, product_a)

    outgoing[...] = jnp.zeros_like(outgoing)
    total = spread[:48] + spread[48:]
    for c in range(3):
        for r in range(28):
            at = c * 8 + r % 7
            outgoing[r // 7, at : at + 1, :] = total[
                c * 16 + r // 2 : c * 16 + r // 2 + 1, (r % 2) * LANES : (r % 2 + 1) * LANES
            ]
    copies = []
    for i, (device, slot) in enumerate(((left, 0), (right, 2), (far, 3))):
        copies.append(
            send(outgoing.at[slot], terms.at[i], term_send.at[i], term_recv.at[i], {"graph": device})
        )
    for copy in copies:
        copy.wait()
    forces = incoming[...] - (outgoing[1] + terms[0] + terms[1] + terms[2])
    miss = forces - wanted[...]
    backs[1] = 2.0 * weight_loss * miss
    copies = []
    for i, (device, slot) in enumerate(((left, 2), (right, 0), (far, 3))):
        copies.append(
            send(backs.at[1], backs.at[slot], term_send.at[3 + i], term_recv.at[3 + i], {"graph": device})
        )
    for c in range(3):
        for n in range(tiles):
            forces_ref[c, :, n * LANES : (n + 1) * LANES] = forces[8 * c + n : 8 * c + n + 1, :]
    loss = weight_loss * jnp.sum(miss * miss, axis=(0, 1), keepdims=True)
    for copy in copies:
        copy.wait()

    def coefficients(n, table_rows, plain_coef, slope_coef, wants):
        source_back = pick_three(backs, table_rows, lanes[n], rows_of[n])
        lam = jnp.zeros((PAD, LANES), F32)
        for c in range(3):
            lam = lam + (backs[1, pl.ds(8 * c + n, 1), :] - source_back[c]) * scalar[
                n, c * PAD : (c + 1) * PAD
            ]
        lam = 0.2 * lam
        first, second = node_terms(agg_keep[n])
        w_out = w_out_t[...]
        readout = first * w_out
        dread = jnp.zeros((channels, LANES), F32)
        for j in range(DEG):
            at = slice(j * LANES, (j + 1) * LANES)
            dread = dread + lam[j : j + 1] * (
                query_keep[n, :, at].astype(F32) * slope_keep[n, :, at].astype(F32)
            )
        grad_out[...] += dread * first
        plain = 0.2 * dread * w_out * second
        for j in range(DEG):
            at = slice(j * LANES, (j + 1) * LANES)
            over_slope = lam[j : j + 1] * readout
            query = query_keep[n, :, at].astype(F32)
            plain_coef[:, at] = (plain * query).astype(BF16)
            slope_coef[:, at] = (over_slope * query).astype(BF16)
            wants[:, at] = (
                over_slope * slope_keep[n, :, at].astype(F32)
                + plain * radial_keep[n, :, at].astype(F32)
            ).astype(BF16)

    def products(n, kept, plain_coef, slope_coef, wants):
        grad_radial[...] += lax.dot_general(
            plain_coef[...], kept[0], NT, preferred_element_type=F32
        ) + lax.dot_general(slope_coef[...], kept[1], NT, preferred_element_type=F32)
        grad_source[...] += lax.dot_general(
            rows_keep[n], wants[...], NT, preferred_element_type=F32
        )

    coef_a = (onehots_a.at[:channels], onehots_a.at[channels : 2 * channels], wants_a)
    coef_b = (onehots_b.at[:channels], onehots_b.at[channels : 2 * channels], wants_b)
    for ref in coef_b:
        ref[...] = jnp.zeros_like(ref)

    def two_backward(i, unused):
        n = 2 * i + 1
        products(n - 1, basis_b.at[lax.max(i - 1, 0)], *coef_b)
        coefficients(n, 21, *coef_a)
        products(n, basis_a.at[i], *coef_a)
        coefficients(n + 1, 21, *coef_b)
        return unused

    lax.fori_loop(0, (tiles - 1) // 2, two_backward, 0)
    products(tiles - 1, basis_b.at[tiles // 2 - 1], *coef_b)
    coefficients(0, 28, *coef_a)
    products(0, basis_a.at[tiles // 2], *coef_a)

    radial = grad_radial[...].T
    source = grad_source[...]
    for i in range(groups):
        for k in range(3):
            at = (3 * i + k) * 8
            own[i, 8 * k : 8 * k + 8] = (
                radial[at : at + 8] if at < count else source[at - count : at - count + 8]
            )
        own[i, 24:] = jnp.zeros((8, LANES), F32)
    own[0, 24:25] = jnp.sum(grad_out[...].T, axis=0, keepdims=True)
    own[0, 25:26] = jnp.broadcast_to(loss, (1, LANES))
    copies = []
    for i, p in enumerate(peers):
        copies.append(send(own.at[p], pieces.at[i], piece_send.at[i], piece_recv.at[i], {"graph": p}))
    for copy in copies:
        copy.wait()
    total = own[me]
    for i in range(groups - 1):
        total = total + pieces[i]
    part[batch] = total
    copies = []
    for i, b in enumerate(others):
        copies.append(send(part.at[batch], part.at[batch], part_send.at[i], part_recv.at[i], {"dp": b}))
    for copy in copies:
        copy.wait()
    total = part[0]
    for i in range(1, batches):
        total = total + part[i]
    whole[me] = total
    copies = []
    for i, p in enumerate(peers):
        copies.append(send(whole.at[me], whole.at[me], whole_send.at[i], whole_recv.at[i], {"graph": p}))
    for copy in copies:
        copy.wait()
    whole_ref[...] = whole[...]


def output_kernel(whole_ref, from_ref, forces_ref, radial_ref, source_ref, out_ref, loss_ref):
    count = radial_ref.shape[0]
    for i in range(whole_ref.shape[0]):
        for k in range(3):
            at = (3 * i + k) * 8
            if at < count:
                radial_ref[at : at + 8] = whole_ref[i, 8 * k : 8 * k + 8]
            else:
                source_ref[at - count : at - count + 8] = whole_ref[i, 8 * k : 8 * k + 8]
    out_ref[...] = whole_ref[0, 24:25]
    loss_ref[...] = whole_ref[0, 25:26, :1]
    forces_ref[...] = from_ref[...]


def whole_vmem():
    return pl.BlockSpec(memory_space=VMEM)


def local(
    node_state,
    atom_types,
    positions,
    force_ref,
    edge_source,
    edge_count,
    type_table,
    w_rad,
    w_src,
    w_out,
):
    nodes, channels = node_state.shape[1:]
    groups = lax.axis_size("graph")
    batches = lax.axis_size("dp")
    weight_loss = 1.0 / math.sqrt(3.0 * nodes * groups * node_state.shape[0] * batches)
    count = w_rad.shape[0]
    tiles = nodes // LANES
    wide = DEG * LANES
    dma = pltpu.SemaphoreType.DMA

    def shape(*dims, dtype=F32):
        return jax.ShapeDtypeStruct(dims, dtype)

    others = max(batches - 1, 1)
    forces, whole = pl.pallas_call(
        functools.partial(fused_kernel, groups, batches, weight_loss),
        out_shape=(shape(3, 1, nodes), shape(groups, 32, LANES)),
        in_specs=[whole_vmem()] * 10,
        out_specs=(whole_vmem(),) * 2,
        scratch_shapes=[
            VMEM((4, channels, nodes), BF16),
            VMEM((4, PAD, LANES), F32),
            VMEM((14 * channels, 256), BF16),
            VMEM((channels, count), BF16),
            VMEM((channels, channels), BF16),
            VMEM((channels, LANES), F32),
            VMEM((count, LANES), F32),
            VMEM((tiles, PAD, LANES), jnp.int32),
            VMEM((tiles, PAD, LANES), jnp.int32),
            VMEM((tiles, 2 * PAD, LANES), F32),
            VMEM((16, LANES), F32),
            VMEM((tiles, 4 * PAD, LANES), F32),
            VMEM((tiles // 2 + 1, 2, count, wide), BF16),
            VMEM((tiles // 2, 2, count, wide), BF16),
            VMEM((tiles, channels, wide), BF16),
            VMEM((tiles, channels, wide), BF16),
            VMEM((tiles, channels, wide), BF16),
            VMEM((tiles, channels, wide), BF16),
            VMEM((tiles, channels, LANES), F32),
            *[VMEM((256, wide), BF16)] * 2,
            *[VMEM((channels, wide), F32)] * 2,
            VMEM((96, 256), F32),
            VMEM((PAD, LANES), F32),
            VMEM((4, PAD, LANES), F32),
            VMEM((3, PAD, LANES), F32),
            VMEM((PAD, LANES), F32),
            VMEM((4, PAD, LANES), F32),
            *[VMEM((channels, wide), BF16)] * 2,
            VMEM((channels, count), F32),
            VMEM((channels, channels), F32),
            VMEM((channels, LANES), F32),
            VMEM((groups, 32, LANES), F32),
            VMEM((groups - 1, 32, LANES), F32),
            VMEM((batches, 32, LANES), F32),
            VMEM((groups, 32, LANES), F32),
            dma((6,)),
            dma((6,)),
            dma((6,)),
            dma((6,)),
            dma((groups - 1,)),
            dma((groups - 1,)),
            dma((others,)),
            dma((others,)),
            dma((groups - 1,)),
            dma((groups - 1,)),
        ],
        compiler_params=pltpu.CompilerParams(
            collective_id=0, has_side_effects=True, vmem_limit_bytes=LIMIT
        ),
        name="fused",
    )(
        node_state[0],
        atom_types,
        positions.transpose(1, 0, 2),
        force_ref.transpose(1, 0, 2),
        edge_source,
        edge_count,
        type_table,
        w_rad,
        w_src,
        w_out.reshape(1, channels),
    )
    forces, grad_radial, grad_source, grad_out, loss = pl.pallas_call(
        output_kernel,
        out_shape=(
            shape(3, 1, nodes),
            shape(count, channels),
            shape(channels, channels),
            shape(1, channels),
            shape(1, 1),
        ),
        in_specs=[whole_vmem()] * 2,
        out_specs=(whole_vmem(),) * 5,
        name="output",
    )(whole, forces)
    return forces.transpose(1, 0, 2), grad_radial, grad_source, grad_out[0], loss[0, 0]


def solution(mesh):
    in_specs = (
        P("dp", "graph", None),
        P("dp", "graph"),
        P("dp", None, "graph"),
        P("dp", None, "graph"),
        P("dp", "graph"),
        P("dp", "graph"),
        P(),
        P(),
        P(),
        P(),
    )
    out_specs = (P("dp", None, "graph"), P(), P(), P(), P())
    return jax.shard_map(local, mesh=mesh, in_specs=in_specs, out_specs=out_specs, check_vma=False)
```

```python
import functools
import math

import jax
import jax.numpy as jnp
from jax import lax
from jax.experimental import pallas as pl
from jax.experimental.pallas import tpu as pltpu
from jax.sharding import PartitionSpec as P

MESH = pl.DeviceIdType.MESH
F32 = jnp.float32
BF16 = jnp.bfloat16
NT = (((1,), (1,)), ((), ()))
DEG = 20
PAD = 24
LANES = 128
VMEM = pltpu.VMEM
LIMIT = 62 * 1024 * 1024
WIDE = DEG * LANES
NEAR = 16


def partners(groups):
    me = lax.axis_index("graph")
    left = lax.rem(me + groups - 1, groups)
    right = lax.rem(me + 1, groups)
    far = lax.rem(me + groups // 2, groups)
    return left, right, far


def greet(devices):
    barrier = pltpu.get_barrier_semaphore()
    for device in devices:
        pl.semaphore_signal(barrier, inc=1, device_id=device, device_id_type=MESH)
    pl.semaphore_wait(barrier, len(devices))


def send(src, dst, send_sem, recv_sem, device):
    copy = pltpu.make_async_remote_copy(
        src_ref=src,
        dst_ref=dst,
        send_sem=send_sem,
        recv_sem=recv_sem,
        device_id=device,
        device_id_type=MESH,
    )
    copy.start()
    return copy


def lane_pick(row, index):
    return jnp.take_along_axis(
        jnp.broadcast_to(row, index.shape), index, axis=1, mode="promise_in_bounds"
    )


def pick_three(tab_ref, rows, lane, row_of):
    results = []
    for g in range(0, lane.shape[0], 8):
        lanes_here, row_here = lane[g : g + 8], row_of[g : g + 8]
        result = [jnp.zeros(lanes_here.shape, F32)] * 3
        for r in range(rows):
            here = row_here == r
            for c in range(3):
                at = c * 8 + r % 7
                result[c] = jnp.where(
                    here, lane_pick(tab_ref[r // 7, at : at + 1, :], lanes_here), result[c]
                )
        results.append(result)
    return [jnp.concatenate([result[c] for result in results], axis=0) for c in range(3)]


def basis(dist_row, scaled_centers, gamma):
    diff = (-2.0 * gamma) * dist_row - scaled_centers
    bump = jnp.exp(diff * diff * (-1.0 / (4.0 * gamma)))
    return bump.astype(BF16), (diff * bump).astype(BF16)


def centers(count):
    gamma = count * count / 1152.0
    number = lax.broadcasted_iota(jnp.int32, (count, LANES), 0).astype(F32)
    return number * (12.0 / count) * (-2.0 * gamma), gamma


def node_terms(agg):
    sig = jax.nn.sigmoid(agg)
    first = sig * (1.0 + agg * (1.0 - sig))
    second = sig * (1.0 - sig) * (2.0 + agg * (1.0 - 2.0 * sig))
    return first, second


def prepare_indices(
    groups, source_ref, count_ref, lanes_ref, rows_ref, pick_ref, compact_ref, tiles
):
    me = lax.axis_index("graph")
    slot = lax.broadcasted_iota(jnp.int32, (PAD, LANES), 1) * DEG + lax.broadcasted_iota(
        jnp.int32, (PAD, LANES), 0
    )
    lane = slot & (LANES - 1)
    row_of = slot >> 7
    nodes = tiles * LANES
    for n in range(tiles):
        source = jnp.zeros((PAD, LANES), jnp.int32)
        for r in range(DEG):
            at = (n * DEG + r) * LANES
            source = jnp.where(row_of == r, lane_pick(source_ref[:, at : at + LANES], lane), source)
        block = (source * 74899) >> 26
        offset = (block - me + groups) & (groups - 1)
        position = jnp.where(
            offset == groups - 1, 0, jnp.where(offset == 0, 1, jnp.where(offset == 1, 2, 3))
        )
        picked = position * nodes + source - block * nodes
        live = slot + n * (DEG * LANES) < count_ref[...]
        lanes_ref[n] = picked & (LANES - 1)
        rows_ref[n] = picked >> 7
        pick_ref[n, :PAD] = jnp.where(live, (picked & 255).astype(F32), -1.0)
        pick_ref[n, PAD:] = (picked >> 8).astype(F32)
    lane = lax.broadcasted_iota(jnp.int32, (8, LANES), 1)
    here = (lane >> 4) == lax.broadcasted_iota(jnp.int32, (8, LANES), 0)
    for g in range(2):
        for r in range(PAD // 8):
            values = pick_ref[0, g * PAD + 8 * r : g * PAD + 8 * r + 8]
            values = jnp.take_along_axis(
                values, LANES - NEAR + (lane & (NEAR - 1)), axis=1, mode="promise_in_bounds"
            )
            compact_ref[8 * g + r : 8 * g + r + 1] = jnp.sum(
                jnp.where(here, values, 0.0), axis=0, keepdims=True
            )


def fused_kernel(
    groups,
    batches,
    weight_loss,
    state_ref,
    types_ref,
    place_ref,
    wanted_ref,
    source_ref,
    count_ref,
    table_ref,
    w_rad_ref,
    w_src_ref,
    w_out_ref,
    forces_ref,
    whole_ref,
    states,
    places,
    stack,
    w_rad_t,
    w_src_t,
    w_out_t,
    centre,
    lanes,
    rows_of,
    pick,
    compact,
    scalar,
    basis_a,
    basis_b,
    rows_keep,
    query_keep,
    slope_keep,
    radial_keep,
    agg_keep,
    onehots_a,
    onehots_b,
    product_a,
    product_b,
    spread,
    incoming,
    outgoing,
    terms,
    wanted,
    backs,
    wants_a,
    wants_b,
    grad_radial,
    grad_source,
    grad_out,
    own,
    pieces,
    part,
    whole,
    halo_send,
    halo_recv,
    term_send,
    term_recv,
    piece_send,
    piece_recv,
    part_send,
    part_recv,
    whole_send,
    whole_recv,
):
    nodes, channels = state_ref.shape
    tiles = nodes // LANES
    kinds = table_ref.shape[0]
    count = w_rad_ref.shape[0]
    gamma = count * count / 1152.0
    me = lax.axis_index("graph")
    batch = lax.axis_index("dp")
    left, right, far = partners(groups)
    near_by = (left, right, far)
    peers = [lax.rem(me + d, groups) for d in range(1, groups)]
    others = [lax.rem(batch + d, batches) for d in range(1, batches)]

    barrier = pltpu.get_barrier_semaphore()
    for device in [{"graph": p} for p in peers] + [{"dp": b} for b in others]:
        pl.semaphore_signal(barrier, inc=1, device_id=device, device_id_type=MESH)

    places[1] = jnp.zeros((PAD, LANES), F32)
    for c in range(3):
        for n in range(tiles):
            at = slice(n * LANES, (n + 1) * LANES)
            places[1, 8 * c + n : 8 * c + n + 1, :] = place_ref[c, :, at]
    pl.semaphore_wait(barrier, len(peers) + len(others))
    targets = ((left, 2), (right, 0), (far, 3))
    place_copies, state_copies = [], []
    for i, (device, slot) in enumerate(targets):
        place_copies.append(
            send(places.at[1], places.at[slot], halo_send.at[i], halo_recv.at[i], {"graph": device})
        )
    kind = (types_ref[...] == lax.broadcasted_iota(jnp.int32, (kinds, nodes), 0)).astype(BF16)
    embedded = lax.dot_general(
        table_ref[...], kind, (((0,), (0,)), ((), ())), preferred_element_type=F32
    )
    states[1] = (state_ref[...].astype(F32).T + embedded).astype(BF16)

    def send_state(i):
        device, slot = targets[i]
        state_copies.append(
            send(
                states.at[1], states.at[slot], halo_send.at[3 + i], halo_recv.at[3 + i], {"graph": device}
            )
        )

    send_state(0)
    send_state(1)

    w_rad_t[...] = w_rad_ref[...].astype(F32).T.astype(BF16)
    w_src_t[...] = w_src_ref[...].astype(F32).T.astype(BF16)
    w_out_t[...] = jnp.broadcast_to(w_out_ref[...], (channels, LANES)).T
    wanted[...] = jnp.zeros_like(wanted)
    for c in range(3):
        for n in range(tiles):
            at = slice(n * LANES, (n + 1) * LANES)
            wanted[8 * c + n : 8 * c + n + 1, :] = wanted_ref[c, :, at]
    centre[...] = centers(count)[0]
    spread[...] = jnp.zeros_like(spread)
    incoming[...] = jnp.zeros_like(incoming)
    grad_radial[...] = jnp.zeros_like(grad_radial)
    grad_source[...] = jnp.zeros_like(grad_source)
    grad_out[...] = jnp.zeros_like(grad_out)
    prepare_indices(groups, source_ref, count_ref, lanes, rows_of, pick, compact, tiles)
    for copy in place_copies:
        copy.wait()
    send_state(2)

    def distances(n, table_rows):
        source_place = pick_three(places, table_rows, lanes[n], rows_of[n])
        delta = [source_place[c] - places[1, pl.ds(8 * c + n, 1), :] for c in range(3)]
        dist = jnp.sqrt(delta[0] * delta[0] + delta[1] * delta[1] + delta[2] * delta[2] + 0.25)
        for c in range(3):
            scalar[n, c * PAD : (c + 1) * PAD] = delta[c] / dist
        scalar[n, 3 * PAD :] = dist

    def bases(n, kept):
        for j in range(DEG):
            at = slice(j * LANES, (j + 1) * LANES)
            bump, slant = basis(scalar[n, 3 * PAD + j : 3 * PAD + j + 1, :], centre[...], gamma)
            kept[0, :, at] = bump
            kept[1, :, at] = slant

    def stack_up(halves):
        for half in halves:
            at = (half % 7) * LANES
            stack[
                (half // 2) * channels : (half // 2 + 1) * channels,
                (half % 2) * LANES : (half % 2 + 1) * LANES,
            ] = states[half // 7, :, at : at + LANES]

    lax.fori_loop(1, tiles, lambda n, u: (distances(n, 21), u)[1], 0)
    distances(0, 28)

    def ahead(i, unused):
        bases(2 * i + 1, basis_a.at[i])
        bases(2 * i + 2, basis_b.at[i])
        return unused

    lax.fori_loop(0, tiles // 2, ahead, 0)
    bases(0, basis_a.at[tiles // 2])
    stack[10 * channels : 11 * channels, LANES:] = jnp.zeros((channels, LANES), BF16)
    for copy in state_copies[:2]:
        copy.wait()
    stack_up(range(21))

    numbers = lax.broadcasted_iota(jnp.int32, (256, LANES), 0).astype(F32)

    def look_up(columns, chosen, first, last):
        ones = jnp.concatenate([(numbers == column).astype(BF16) for column in columns], axis=1)
        hi = jnp.concatenate(chosen, axis=1)
        hi = jnp.broadcast_to(hi, (channels, hi.shape[1]))
        found = jnp.dot(
            stack[first * channels : last * channels], ones, preferred_element_type=F32
        )
        rows = found[:channels]
        for c in range(1, last - first):
            rows = jnp.where(
                hi == float(first + c), found[c * channels : (c + 1) * channels], rows
            )
        return ones, rows

    def gather(n, kept, onehots, product):
        columns = [pick[n, pl.ds(j, 1), :] for j in range(DEG)]
        chosen = [pick[n, pl.ds(PAD + j, 1), :] for j in range(DEG)]
        if isinstance(n, int):
            ones, rows = look_up(columns, chosen, 10, 14)
            _, near = look_up(
                [compact[r : r + 1] for r in range(3)], [compact[8 + r : 9 + r] for r in range(3)], 0, 11
            )
            last = lax.broadcasted_iota(jnp.int32, (channels, LANES), 1) >= LANES - NEAR
            parts = []
            for j in range(DEG):
                moved = pltpu.roll(
                    near[:, (j // 8) * LANES : (j // 8 + 1) * LANES],
                    LANES - NEAR - NEAR * (j % 8),
                    1,
                )
                parts.append(jnp.where(last, moved, rows[:, j * LANES : (j + 1) * LANES]))
            rows = jnp.concatenate(parts, axis=1)
        else:
            ones, rows = look_up(columns, chosen, 0, 11)
        onehots[...] = ones
        rows = rows.astype(BF16)
        rows_keep[n] = rows
        query = jnp.dot(w_src_t[...], rows, preferred_element_type=F32)
        radial = jnp.dot(w_rad_t[...], kept[0], preferred_element_type=F32)
        slope = jnp.dot(w_rad_t[...], kept[1], preferred_element_type=F32)
        query_keep[n] = query.astype(BF16)
        slope_keep[n] = slope.astype(BF16)
        radial_keep[n] = radial.astype(BF16)
        product[...] = query * slope
        term = radial * query
        total = term[:, :LANES]
        for j in range(1, DEG):
            total = total + term[:, j * LANES : (j + 1) * LANES]
        agg_keep[n] = 0.2 * total

    def pull(n, onehots, product):
        first, _ = node_terms(agg_keep[n])
        readout = 0.2 * first * w_out_t[...]
        inward = [jnp.zeros((1, LANES), F32)] * 3
        lhs = []
        chunk = lax.broadcasted_iota(jnp.int32, (16, LANES), 0).astype(F32)
        for j in range(DEG):
            force = jnp.sum(readout * product[:, j * LANES : (j + 1) * LANES], axis=0, keepdims=True)
            here = chunk == pick[n, PAD + j : PAD + j + 1, :]
            high, low = [], []
            for c in range(3):
                moved = force * scalar[n, c * PAD + j : c * PAD + j + 1, :]
                inward[c] = inward[c] + moved
                term = jnp.where(here, moved, 0.0)
                top = term.astype(BF16)
                high.append(top)
                low.append((term - top.astype(F32)).astype(BF16))
            lhs.append(jnp.concatenate(high + low, axis=0))
        lhs = jnp.concatenate(lhs, axis=1)
        spread[...] += lax.dot_general(lhs, onehots[...], NT, preferred_element_type=F32)
        for c in range(3):
            incoming[pl.ds(8 * c + n, 1), :] = inward[c]

    agg_keep[0] = jnp.zeros((channels, LANES), F32)
    product_b[...] = jnp.zeros_like(product_b)
    onehots_b[...] = jnp.zeros_like(onehots_b)

    def two_forward(i, unused):
        n = 2 * i + 1
        pull(n - 1, onehots_b, product_b)
        gather(n, basis_a.at[i], onehots_a, product_a)
        pull(n, onehots_a, product_a)
        gather(n + 1, basis_b.at[i], onehots_b, product_b)
        return unused

    lax.fori_loop(0, (tiles - 1) // 2, two_forward, 0)
    state_copies[2].wait()
    stack_up(range(21, 28))
    pull(tiles - 1, onehots_b, product_b)
    gather(0, basis_a.at[tiles // 2], onehots_a, product_a)
    pull(0, onehots_a, product_a)

    outgoing[...] = jnp.zeros_like(outgoing)
    total = spread[:48] + spread[48:]
    for c in range(3):
        for r in range(28):
            at = c * 8 + r % 7
            outgoing[r // 7, at : at + 1, :] = total[
                c * 16 + r // 2 : c * 16 + r // 2 + 1, (r % 2) * LANES : (r % 2 + 1) * LANES
            ]
    copies = []
    for i, (device, slot) in enumerate(((left, 0), (right, 2), (far, 3))):
        copies.append(
            send(outgoing.at[slot], terms.at[i], term_send.at[i], term_recv.at[i], {"graph": device})
        )
    for copy in copies:
        copy.wait()
    forces = incoming[...] - (outgoing[1] + terms[0] + terms[1] + terms[2])
    miss = forces - wanted[...]
    backs[1] = 2.0 * weight_loss * miss
    copies = []
    for i, (device, slot) in enumerate(((left, 2), (right, 0), (far, 3))):
        copies.append(
            send(backs.at[1], backs.at[slot], term_send.at[3 + i], term_recv.at[3 + i], {"graph": device})
        )
    for c in range(3):
        for n in range(tiles):
            forces_ref[c, :, n * LANES : (n + 1) * LANES] = forces[8 * c + n : 8 * c + n + 1, :]
    loss = weight_loss * jnp.sum(miss * miss, axis=(0, 1), keepdims=True)
    for copy in copies:
        copy.wait()

    def coefficients(n, table_rows, plain_coef, slope_coef, wants):
        source_back = pick_three(backs, table_rows, lanes[n], rows_of[n])
        lam = jnp.zeros((PAD, LANES), F32)
        for c in range(3):
            lam = lam + (backs[1, pl.ds(8 * c + n, 1), :] - source_back[c]) * scalar[
                n, c * PAD : (c + 1) * PAD
            ]
        lam = 0.2 * lam
        first, second = node_terms(agg_keep[n])
        w_out = w_out_t[...]
        readout = first * w_out
        dread = jnp.zeros((channels, LANES), F32)
        for j in range(DEG):
            at = slice(j * LANES, (j + 1) * LANES)
            dread = dread + lam[j : j + 1] * (
                query_keep[n, :, at].astype(F32) * slope_keep[n, :, at].astype(F32)
            )
        grad_out[...] += dread * first
        plain = 0.2 * dread * w_out * second
        for j in range(DEG):
            at = slice(j * LANES, (j + 1) * LANES)
            over_slope = lam[j : j + 1] * readout
            query = query_keep[n, :, at].astype(F32)
            plain_coef[:, at] = (plain * query).astype(BF16)
            slope_coef[:, at] = (over_slope * query).astype(BF16)
            wants[:, at] = (
                over_slope * slope_keep[n, :, at].astype(F32)
                + plain * radial_keep[n, :, at].astype(F32)
            ).astype(BF16)

    def products(n, kept, plain_coef, slope_coef, wants):
        grad_radial[...] += lax.dot_general(
            plain_coef[...], kept[0], NT, preferred_element_type=F32
        ) + lax.dot_general(slope_coef[...], kept[1], NT, preferred_element_type=F32)
        grad_source[...] += lax.dot_general(
            rows_keep[n], wants[...], NT, preferred_element_type=F32
        )

    coef_a = (onehots_a.at[:channels], onehots_a.at[channels : 2 * channels], wants_a)
    coef_b = (onehots_b.at[:channels], onehots_b.at[channels : 2 * channels], wants_b)
    for ref in coef_b:
        ref[...] = jnp.zeros_like(ref)

    def two_backward(i, unused):
        n = 2 * i + 1
        products(n - 1, basis_b.at[lax.max(i - 1, 0)], *coef_b)
        coefficients(n, 21, *coef_a)
        products(n, basis_a.at[i], *coef_a)
        coefficients(n + 1, 21, *coef_b)
        return unused

    lax.fori_loop(0, (tiles - 1) // 2, two_backward, 0)
    products(tiles - 1, basis_b.at[tiles // 2 - 1], *coef_b)
    coefficients(0, 28, *coef_a)
    products(0, basis_a.at[tiles // 2], *coef_a)

    def parts_of(value, number):
        parts = []
        for _ in range(number):
            part = value.astype(BF16).astype(F32)
            parts.append(part)
            value = value - part
        return parts

    def piece_of(rows, out, loss):
        more = parts_of(out, 2) + parts_of(loss, 3) + [jnp.zeros((3, LANES), F32)]
        return jnp.concatenate([rows] + more, axis=0)

    radial = grad_radial[...].T
    source = grad_source[...]
    nothing = jnp.zeros((1, LANES), F32)
    for i in range(groups):
        rows = [
            radial[at : at + 8] if at < count else source[at - count : at - count + 8]
            for at in range(24 * i, 24 * i + 24, 8)
        ]
        out = nothing if i else jnp.sum(grad_out[...].T, axis=0, keepdims=True)
        total = nothing if i else jnp.broadcast_to(loss, (1, LANES))
        own[i] = piece_of(jnp.concatenate(rows, axis=0), out, total).astype(BF16)
    copies = []
    for i, p in enumerate(peers):
        copies.append(send(own.at[p], pieces.at[i], piece_send.at[i], piece_recv.at[i], {"graph": p}))
    for copy in copies:
        copy.wait()
    total = own[me].astype(F32)
    for i in range(groups - 1):
        total = total + pieces[i].astype(F32)
    part[batch] = total
    copies = []
    for i, b in enumerate(others):
        copies.append(send(part.at[batch], part.at[batch], part_send.at[i], part_recv.at[i], {"dp": b}))
    for copy in copies:
        copy.wait()
    total = part[0]
    for i in range(1, batches):
        total = total + part[i]
    whole[me] = piece_of(
        total[:24], total[24:25] + total[25:26], total[26:27] + total[27:28] + total[28:29]
    ).astype(BF16)
    copies = []
    for i, p in enumerate(peers):
        copies.append(send(whole.at[me], whole.at[me], whole_send.at[i], whole_recv.at[i], {"graph": p}))
    for copy in copies:
        copy.wait()
    whole_ref[...] = whole[...]


def output_kernel(whole_ref, from_ref, forces_ref, radial_ref, source_ref, out_ref, loss_ref):
    count = radial_ref.shape[0]
    for i in range(whole_ref.shape[0]):
        piece = whole_ref[i].astype(F32)
        for k in range(3):
            at = (3 * i + k) * 8
            if at < count:
                radial_ref[at : at + 8] = piece[8 * k : 8 * k + 8]
            else:
                source_ref[at - count : at - count + 8] = piece[8 * k : 8 * k + 8]
        if i == 0:
            out_ref[...] = piece[24:25] + piece[25:26]
            loss_ref[...] = (piece[26:27] + piece[27:28] + piece[28:29])[:, :1]
    forces_ref[...] = from_ref[...]


def whole_vmem():
    return pl.BlockSpec(memory_space=VMEM)


def local(
    node_state,
    atom_types,
    positions,
    force_ref,
    edge_source,
    edge_count,
    type_table,
    w_rad,
    w_src,
    w_out,
):
    nodes, channels = node_state.shape[1:]
    groups = lax.axis_size("graph")
    batches = lax.axis_size("dp")
    weight_loss = 1.0 / math.sqrt(3.0 * nodes * groups * node_state.shape[0] * batches)
    count = w_rad.shape[0]
    tiles = nodes // LANES
    wide = DEG * LANES
    dma = pltpu.SemaphoreType.DMA

    def shape(*dims, dtype=F32):
        return jax.ShapeDtypeStruct(dims, dtype)

    others = max(batches - 1, 1)
    forces, whole = pl.pallas_call(
        functools.partial(fused_kernel, groups, batches, weight_loss),
        out_shape=(shape(3, 1, nodes), shape(groups, 32, LANES, dtype=BF16)),
        in_specs=[whole_vmem()] * 10,
        out_specs=(whole_vmem(),) * 2,
        scratch_shapes=[
            VMEM((4, channels, nodes), BF16),
            VMEM((4, PAD, LANES), F32),
            VMEM((14 * channels, 256), BF16),
            VMEM((channels, count), BF16),
            VMEM((channels, channels), BF16),
            VMEM((channels, LANES), F32),
            VMEM((count, LANES), F32),
            VMEM((tiles, PAD, LANES), jnp.int32),
            VMEM((tiles, PAD, LANES), jnp.int32),
            VMEM((tiles, 2 * PAD, LANES), F32),
            VMEM((16, LANES), F32),
            VMEM((tiles, 4 * PAD, LANES), F32),
            VMEM((tiles // 2 + 1, 2, count, wide), BF16),
            VMEM((tiles // 2, 2, count, wide), BF16),
            VMEM((tiles, channels, wide), BF16),
            VMEM((tiles, channels, wide), BF16),
            VMEM((tiles, channels, wide), BF16),
            VMEM((tiles, channels, wide), BF16),
            VMEM((tiles, channels, LANES), F32),
            *[VMEM((256, wide), BF16)] * 2,
            *[VMEM((channels, wide), F32)] * 2,
            VMEM((96, 256), F32),
            VMEM((PAD, LANES), F32),
            VMEM((4, PAD, LANES), F32),
            VMEM((3, PAD, LANES), F32),
            VMEM((PAD, LANES), F32),
            VMEM((4, PAD, LANES), F32),
            *[VMEM((channels, wide), BF16)] * 2,
            VMEM((channels, count), F32),
            VMEM((channels, channels), F32),
            VMEM((channels, LANES), F32),
            VMEM((groups, 32, LANES), BF16),
            VMEM((groups - 1, 32, LANES), BF16),
            VMEM((batches, 32, LANES), F32),
            VMEM((groups, 32, LANES), BF16),
            dma((6,)),
            dma((6,)),
            dma((6,)),
            dma((6,)),
            dma((groups - 1,)),
            dma((groups - 1,)),
            dma((others,)),
            dma((others,)),
            dma((groups - 1,)),
            dma((groups - 1,)),
        ],
        compiler_params=pltpu.CompilerParams(
            collective_id=0, has_side_effects=True, vmem_limit_bytes=LIMIT
        ),
        name="fused",
    )(
        node_state[0],
        atom_types,
        positions.transpose(1, 0, 2),
        force_ref.transpose(1, 0, 2),
        edge_source,
        edge_count,
        type_table,
        w_rad,
        w_src,
        w_out.reshape(1, channels),
    )
    forces, grad_radial, grad_source, grad_out, loss = pl.pallas_call(
        output_kernel,
        out_shape=(
            shape(3, 1, nodes),
            shape(count, channels),
            shape(channels, channels),
            shape(1, channels),
            shape(1, 1),
        ),
        in_specs=[whole_vmem()] * 2,
        out_specs=(whole_vmem(),) * 5,
        name="output",
    )(whole, forces)
    return forces.transpose(1, 0, 2), grad_radial, grad_source, grad_out[0], loss[0, 0]


def solution(mesh):
    in_specs = (
        P("dp", "graph", None),
        P("dp", "graph"),
        P("dp", None, "graph"),
        P("dp", None, "graph"),
        P("dp", "graph"),
        P("dp", "graph"),
        P(),
        P(),
        P(),
        P(),
    )
    out_specs = (P("dp", None, "graph"), P(), P(), P(), P())
    return jax.shard_map(local, mesh=mesh, in_specs=in_specs, out_specs=out_specs, check_vma=False)
```

```python
import functools
import math

import jax
import jax.numpy as jnp
from jax import lax
from jax.experimental import pallas as pl
from jax.experimental.pallas import tpu as pltpu
from jax.sharding import PartitionSpec as P

MESH = pl.DeviceIdType.MESH
F32 = jnp.float32
BF16 = jnp.bfloat16
NT = (((1,), (1,)), ((), ()))
DEG = 20
PAD = 24
LANES = 128
VMEM = pltpu.VMEM
LIMIT = 62 * 1024 * 1024
WIDE = DEG * LANES
NEAR = 16


def partners(groups):
    me = lax.axis_index("graph")
    left = lax.rem(me + groups - 1, groups)
    right = lax.rem(me + 1, groups)
    far = lax.rem(me + groups // 2, groups)
    return left, right, far


def farthest_first(count):
    if count == 16:
        return [4, 12, 5, 11, 3, 13, 6, 10, 2, 14, 7, 9, 8, 1, 15]
    if count == 8:
        return [3, 5, 4, 1, 7, 2, 6]
    return list(range(1, count))


def send(src, dst, send_sem, recv_sem, device):
    copy = pltpu.make_async_remote_copy(
        src_ref=src,
        dst_ref=dst,
        send_sem=send_sem,
        recv_sem=recv_sem,
        device_id=device,
        device_id_type=MESH,
    )
    copy.start()
    return copy


def lane_pick(row, index):
    return jnp.take_along_axis(
        jnp.broadcast_to(row, index.shape), index, axis=1, mode="promise_in_bounds"
    )


def pick_three(tab_ref, rows, lane, row_of):
    results = []
    for g in range(0, lane.shape[0], 8):
        lanes_here, row_here = lane[g : g + 8], row_of[g : g + 8]
        result = [jnp.zeros(lanes_here.shape, F32)] * 3
        for r in range(rows):
            here = row_here == r
            for c in range(3):
                at = c * 8 + r % 7
                result[c] = jnp.where(
                    here, lane_pick(tab_ref[r // 7, at : at + 1, :], lanes_here), result[c]
                )
        results.append(result)
    return [jnp.concatenate([result[c] for result in results], axis=0) for c in range(3)]


def basis(dist_row, scaled_centers, gamma):
    diff = (-2.0 * gamma) * dist_row - scaled_centers
    bump = jnp.exp(diff * diff * (-1.0 / (4.0 * gamma)))
    return bump.astype(BF16), (diff * bump).astype(BF16)


def centers(count):
    gamma = count * count / 1152.0
    number = lax.broadcasted_iota(jnp.int32, (count, LANES), 0).astype(F32)
    return number * (12.0 / count) * (-2.0 * gamma), gamma


def node_terms(agg):
    sig = jax.nn.sigmoid(agg)
    first = sig * (1.0 + agg * (1.0 - sig))
    second = sig * (1.0 - sig) * (2.0 + agg * (1.0 - 2.0 * sig))
    return first, second


def prepare_indices(
    groups, source_ref, count_ref, lanes_ref, rows_ref, pick_ref, compact_ref, tiles
):
    me = lax.axis_index("graph")
    slot = lax.broadcasted_iota(jnp.int32, (PAD, LANES), 1) * DEG + lax.broadcasted_iota(
        jnp.int32, (PAD, LANES), 0
    )
    lane = slot & (LANES - 1)
    row_of = slot >> 7
    nodes = tiles * LANES
    for n in range(tiles):
        source = jnp.zeros((PAD, LANES), jnp.int32)
        for r in range(DEG):
            at = (n * DEG + r) * LANES
            source = jnp.where(row_of == r, lane_pick(source_ref[:, at : at + LANES], lane), source)
        block = (source * 74899) >> 26
        offset = (block - me + groups) & (groups - 1)
        position = jnp.where(
            offset == groups - 1, 0, jnp.where(offset == 0, 1, jnp.where(offset == 1, 2, 3))
        )
        picked = position * nodes + source - block * nodes
        live = slot + n * (DEG * LANES) < count_ref[...]
        lanes_ref[n] = picked & (LANES - 1)
        rows_ref[n] = picked >> 7
        pick_ref[n, :PAD] = jnp.where(live, (picked & 255).astype(F32), -1.0)
        pick_ref[n, PAD:] = (picked >> 8).astype(F32)
    lane = lax.broadcasted_iota(jnp.int32, (8, LANES), 1)
    here = (lane >> 4) == lax.broadcasted_iota(jnp.int32, (8, LANES), 0)
    for g in range(2):
        for r in range(PAD // 8):
            values = pick_ref[0, g * PAD + 8 * r : g * PAD + 8 * r + 8]
            values = jnp.take_along_axis(
                values, LANES - NEAR + (lane & (NEAR - 1)), axis=1, mode="promise_in_bounds"
            )
            compact_ref[8 * g + r : 8 * g + r + 1] = jnp.sum(
                jnp.where(here, values, 0.0), axis=0, keepdims=True
            )


def fused_kernel(
    groups,
    batches,
    weight_loss,
    state_ref,
    types_ref,
    place_ref,
    wanted_ref,
    source_ref,
    count_ref,
    table_ref,
    w_rad_ref,
    w_src_ref,
    w_out_ref,
    forces_ref,
    whole_ref,
    states,
    places,
    stack,
    w_rad_t,
    w_src_t,
    w_out_t,
    centre,
    lanes,
    rows_of,
    pick,
    compact,
    scalar,
    basis_a,
    basis_b,
    rows_keep,
    query_keep,
    slope_keep,
    radial_keep,
    agg_keep,
    onehots_a,
    onehots_b,
    product_a,
    product_b,
    spread,
    incoming,
    outgoing,
    terms,
    wanted,
    backs,
    wants_a,
    wants_b,
    grad_radial,
    grad_source,
    grad_out,
    own,
    pieces,
    part,
    whole,
    halo_send,
    halo_recv,
    term_send,
    term_recv,
    piece_send,
    piece_recv,
    part_send,
    part_recv,
    whole_send,
    whole_recv,
):
    nodes, channels = state_ref.shape
    tiles = nodes // LANES
    kinds = table_ref.shape[0]
    count = w_rad_ref.shape[0]
    gamma = count * count / 1152.0
    me = lax.axis_index("graph")
    batch = lax.axis_index("dp")
    left, right, far = partners(groups)
    near_by = (left, right, far)
    peers = [lax.rem(me + d, groups) for d in farthest_first(groups)]
    others = [lax.rem(batch + d, batches) for d in farthest_first(batches)]

    barrier = pltpu.get_barrier_semaphore()
    for device in [{"graph": p} for p in peers] + [{"dp": b} for b in others]:
        pl.semaphore_signal(barrier, inc=1, device_id=device, device_id_type=MESH)

    places[1] = jnp.zeros((PAD, LANES), F32)
    for c in range(3):
        for n in range(tiles):
            at = slice(n * LANES, (n + 1) * LANES)
            places[1, 8 * c + n : 8 * c + n + 1, :] = place_ref[c, :, at]
    pl.semaphore_wait(barrier, len(peers) + len(others))
    targets = ((left, 2), (right, 0), (far, 3))
    place_copies, state_copies = [], []
    for i, (device, slot) in enumerate(targets):
        place_copies.append(
            send(places.at[1], places.at[slot], halo_send.at[i], halo_recv.at[i], {"graph": device})
        )
    kind = (types_ref[...] == lax.broadcasted_iota(jnp.int32, (kinds, nodes), 0)).astype(BF16)
    embedded = lax.dot_general(
        table_ref[...], kind, (((0,), (0,)), ((), ())), preferred_element_type=F32
    )
    states[1] = (state_ref[...].astype(F32).T + embedded).astype(BF16)

    def send_state(i):
        device, slot = targets[i]
        state_copies.append(
            send(
                states.at[1], states.at[slot], halo_send.at[3 + i], halo_recv.at[3 + i], {"graph": device}
            )
        )

    send_state(0)
    send_state(1)

    w_rad_t[...] = w_rad_ref[...].astype(F32).T.astype(BF16)
    w_src_t[...] = w_src_ref[...].astype(F32).T.astype(BF16)
    w_out_t[...] = jnp.broadcast_to(w_out_ref[...], (channels, LANES)).T
    wanted[...] = jnp.zeros_like(wanted)
    for c in range(3):
        for n in range(tiles):
            at = slice(n * LANES, (n + 1) * LANES)
            wanted[8 * c + n : 8 * c + n + 1, :] = wanted_ref[c, :, at]
    centre[...] = centers(count)[0]
    spread[...] = jnp.zeros_like(spread)
    incoming[...] = jnp.zeros_like(incoming)
    grad_radial[...] = jnp.zeros_like(grad_radial)
    grad_source[...] = jnp.zeros_like(grad_source)
    grad_out[...] = jnp.zeros_like(grad_out)
    prepare_indices(groups, source_ref, count_ref, lanes, rows_of, pick, compact, tiles)
    for copy in place_copies:
        copy.wait()
    send_state(2)

    def distances(n, table_rows):
        source_place = pick_three(places, table_rows, lanes[n], rows_of[n])
        delta = [source_place[c] - places[1, pl.ds(8 * c + n, 1), :] for c in range(3)]
        dist = jnp.sqrt(delta[0] * delta[0] + delta[1] * delta[1] + delta[2] * delta[2] + 0.25)
        for c in range(3):
            scalar[n, c * PAD : (c + 1) * PAD] = delta[c] / dist
        scalar[n, 3 * PAD :] = dist

    def bases(n, kept):
        for j in range(DEG):
            at = slice(j * LANES, (j + 1) * LANES)
            bump, slant = basis(scalar[n, 3 * PAD + j : 3 * PAD + j + 1, :], centre[...], gamma)
            kept[0, :, at] = bump
            kept[1, :, at] = slant

    def stack_up(halves):
        for half in halves:
            at = (half % 7) * LANES
            stack[
                (half // 2) * channels : (half // 2 + 1) * channels,
                (half % 2) * LANES : (half % 2 + 1) * LANES,
            ] = states[half // 7, :, at : at + LANES]

    lax.fori_loop(1, tiles, lambda n, u: (distances(n, 21), u)[1], 0)
    distances(0, 28)

    def ahead(i, unused):
        bases(2 * i + 1, basis_a.at[i])
        bases(2 * i + 2, basis_b.at[i])
        return unused

    lax.fori_loop(0, tiles // 2, ahead, 0)
    bases(0, basis_a.at[tiles // 2])
    stack[10 * channels : 11 * channels, LANES:] = jnp.zeros((channels, LANES), BF16)
    for copy in state_copies[:2]:
        copy.wait()
    stack_up(range(21))

    numbers = lax.broadcasted_iota(jnp.int32, (256, LANES), 0).astype(F32)

    def look_up(columns, chosen, first, last):
        ones = jnp.concatenate([(numbers == column).astype(BF16) for column in columns], axis=1)
        hi = jnp.concatenate(chosen, axis=1)
        hi = jnp.broadcast_to(hi, (channels, hi.shape[1]))
        found = jnp.dot(
            stack[first * channels : last * channels], ones, preferred_element_type=F32
        )
        rows = found[:channels]
        for c in range(1, last - first):
            rows = jnp.where(
                hi == float(first + c), found[c * channels : (c + 1) * channels], rows
            )
        return ones, rows

    def gather(n, kept, onehots, product):
        columns = [pick[n, pl.ds(j, 1), :] for j in range(DEG)]
        chosen = [pick[n, pl.ds(PAD + j, 1), :] for j in range(DEG)]
        if isinstance(n, int):
            ones, rows = look_up(columns, chosen, 10, 14)
            _, near = look_up(
                [compact[r : r + 1] for r in range(3)], [compact[8 + r : 9 + r] for r in range(3)], 0, 11
            )
            last = lax.broadcasted_iota(jnp.int32, (channels, LANES), 1) >= LANES - NEAR
            parts = []
            for j in range(DEG):
                moved = pltpu.roll(
                    near[:, (j // 8) * LANES : (j // 8 + 1) * LANES],
                    LANES - NEAR - NEAR * (j % 8),
                    1,
                )
                parts.append(jnp.where(last, moved, rows[:, j * LANES : (j + 1) * LANES]))
            rows = jnp.concatenate(parts, axis=1)
        else:
            ones, rows = look_up(columns, chosen, 0, 11)
        onehots[...] = ones
        rows = rows.astype(BF16)
        rows_keep[n] = rows
        query = jnp.dot(w_src_t[...], rows, preferred_element_type=F32)
        radial = jnp.dot(w_rad_t[...], kept[0], preferred_element_type=F32)
        slope = jnp.dot(w_rad_t[...], kept[1], preferred_element_type=F32)
        query_keep[n] = query.astype(BF16)
        slope_keep[n] = slope.astype(BF16)
        radial_keep[n] = radial.astype(BF16)
        product[...] = query * slope
        term = radial * query
        total = term[:, :LANES]
        for j in range(1, DEG):
            total = total + term[:, j * LANES : (j + 1) * LANES]
        agg_keep[n] = 0.2 * total

    def pull(n, onehots, product):
        first, _ = node_terms(agg_keep[n])
        readout = 0.2 * first * w_out_t[...]
        inward = [jnp.zeros((1, LANES), F32)] * 3
        lhs = []
        chunk = lax.broadcasted_iota(jnp.int32, (16, LANES), 0).astype(F32)
        for j in range(DEG):
            force = jnp.sum(readout * product[:, j * LANES : (j + 1) * LANES], axis=0, keepdims=True)
            here = chunk == pick[n, PAD + j : PAD + j + 1, :]
            high, low = [], []
            for c in range(3):
                moved = force * scalar[n, c * PAD + j : c * PAD + j + 1, :]
                inward[c] = inward[c] + moved
                term = jnp.where(here, moved, 0.0)
                top = term.astype(BF16)
                high.append(top)
                low.append((term - top.astype(F32)).astype(BF16))
            lhs.append(jnp.concatenate(high + low, axis=0))
        lhs = jnp.concatenate(lhs, axis=1)
        spread[...] += lax.dot_general(lhs, onehots[...], NT, preferred_element_type=F32)
        for c in range(3):
            incoming[pl.ds(8 * c + n, 1), :] = inward[c]

    def two_forward(i, unused):
        n = 2 * i + 1
        pull(n, onehots_a, product_a)
        gather(n + 1, basis_b.at[i], onehots_b, product_b)
        pull(n + 1, onehots_b, product_b)
        gather(n + 2, basis_a.at[i + 1], onehots_a, product_a)
        return unused

    gather(jnp.int32(1), basis_a.at[0], onehots_a, product_a)
    lax.fori_loop(0, (tiles - 3) // 2, two_forward, 0)
    pull(tiles - 2, onehots_a, product_a)
    gather(jnp.int32(tiles - 1), basis_b.at[tiles // 2 - 1], onehots_b, product_b)
    state_copies[2].wait()
    stack_up(range(21, 28))
    pull(tiles - 1, onehots_b, product_b)
    gather(0, basis_a.at[tiles // 2], onehots_a, product_a)
    pull(0, onehots_a, product_a)

    outgoing[...] = jnp.zeros_like(outgoing)
    total = spread[:48] + spread[48:]
    for c in range(3):
        for r in range(28):
            at = c * 8 + r % 7
            outgoing[r // 7, at : at + 1, :] = total[
                c * 16 + r // 2 : c * 16 + r // 2 + 1, (r % 2) * LANES : (r % 2 + 1) * LANES
            ]
    copies = []
    for i, (device, slot) in enumerate(((left, 0), (right, 2), (far, 3))):
        copies.append(
            send(outgoing.at[slot], terms.at[i], term_send.at[i], term_recv.at[i], {"graph": device})
        )
    for copy in copies:
        copy.wait()
    forces = incoming[...] - (outgoing[1] + terms[0] + terms[1] + terms[2])
    miss = forces - wanted[...]
    backs[1] = 2.0 * weight_loss * miss
    copies = []
    for i, (device, slot) in enumerate(((left, 2), (right, 0), (far, 3))):
        copies.append(
            send(backs.at[1], backs.at[slot], term_send.at[3 + i], term_recv.at[3 + i], {"graph": device})
        )
    for c in range(3):
        for n in range(tiles):
            forces_ref[c, :, n * LANES : (n + 1) * LANES] = forces[8 * c + n : 8 * c + n + 1, :]
    loss = weight_loss * jnp.sum(miss * miss, axis=(0, 1), keepdims=True)
    for copy in copies:
        copy.wait()

    def coefficients(n, table_rows, plain_coef, slope_coef, wants):
        source_back = pick_three(backs, table_rows, lanes[n], rows_of[n])
        lam = jnp.zeros((PAD, LANES), F32)
        for c in range(3):
            lam = lam + (backs[1, pl.ds(8 * c + n, 1), :] - source_back[c]) * scalar[
                n, c * PAD : (c + 1) * PAD
            ]
        lam = 0.2 * lam
        first, second = node_terms(agg_keep[n])
        w_out = w_out_t[...]
        readout = first * w_out
        dread = jnp.zeros((channels, LANES), F32)
        for j in range(DEG):
            at = slice(j * LANES, (j + 1) * LANES)
            dread = dread + lam[j : j + 1] * (
                query_keep[n, :, at].astype(F32) * slope_keep[n, :, at].astype(F32)
            )
        grad_out[...] += dread * first
        plain = 0.2 * dread * w_out * second
        for j in range(DEG):
            at = slice(j * LANES, (j + 1) * LANES)
            over_slope = lam[j : j + 1] * readout
            query = query_keep[n, :, at].astype(F32)
            plain_coef[:, at] = (plain * query).astype(BF16)
            slope_coef[:, at] = (over_slope * query).astype(BF16)
            wants[:, at] = (
                over_slope * slope_keep[n, :, at].astype(F32)
                + plain * radial_keep[n, :, at].astype(F32)
            ).astype(BF16)

    def products(n, kept, plain_coef, slope_coef, wants):
        grad_radial[...] += lax.dot_general(
            kept[0], plain_coef[...], NT, preferred_element_type=F32
        ) + lax.dot_general(kept[1], slope_coef[...], NT, preferred_element_type=F32)
        grad_source[...] += lax.dot_general(
            rows_keep[n], wants[...], NT, preferred_element_type=F32
        )

    coef_a = (onehots_a.at[:channels], onehots_a.at[channels : 2 * channels], wants_a)
    coef_b = (onehots_b.at[:channels], onehots_b.at[channels : 2 * channels], wants_b)
    def two_backward(i, unused):
        n = 2 * i + 1
        products(n, basis_a.at[i], *coef_a)
        coefficients(n + 1, 21, *coef_b)
        products(n + 1, basis_b.at[i], *coef_b)
        coefficients(n + 2, 21, *coef_a)
        return unused

    coefficients(1, 21, *coef_a)
    lax.fori_loop(0, (tiles - 3) // 2, two_backward, 0)
    products(tiles - 2, basis_a.at[tiles // 2 - 1], *coef_a)
    coefficients(tiles - 1, 21, *coef_b)
    products(tiles - 1, basis_b.at[tiles // 2 - 1], *coef_b)
    coefficients(0, 28, *coef_a)
    products(0, basis_a.at[tiles // 2], *coef_a)

    def parts_of(value, number):
        parts = []
        for _ in range(number):
            part = value.astype(BF16).astype(F32)
            parts.append(part)
            value = value - part
        return parts

    def piece_of(rows, out, loss):
        more = parts_of(out, 2) + parts_of(loss, 3) + [jnp.zeros((3, LANES), F32)]
        return jnp.concatenate([rows] + more, axis=0)

    radial = grad_radial[...]
    source = grad_source[...]
    nothing = jnp.zeros((1, LANES), F32)
    for i in range(groups):
        rows = [
            radial[at : at + 8] if at < count else source[at - count : at - count + 8]
            for at in range(24 * i, 24 * i + 24, 8)
        ]
        out = nothing if i else jnp.sum(grad_out[...].T, axis=0, keepdims=True)
        total = nothing if i else jnp.broadcast_to(loss, (1, LANES))
        own[i] = piece_of(jnp.concatenate(rows, axis=0), out, total).astype(BF16)
    copies = []
    for i, p in enumerate(peers):
        copies.append(send(own.at[p], pieces.at[i], piece_send.at[i], piece_recv.at[i], {"graph": p}))
    for copy in copies:
        copy.wait()
    total = own[me].astype(F32)
    for i in range(groups - 1):
        total = total + pieces[i].astype(F32)
    part[batch] = total
    copies = []
    for i, b in enumerate(others):
        copies.append(send(part.at[batch], part.at[batch], part_send.at[i], part_recv.at[i], {"dp": b}))
    for copy in copies:
        copy.wait()
    total = part[0]
    for i in range(1, batches):
        total = total + part[i]
    whole[me] = piece_of(
        total[:24], total[24:25] + total[25:26], total[26:27] + total[27:28] + total[28:29]
    ).astype(BF16)
    copies = []
    for i, p in enumerate(peers):
        copies.append(send(whole.at[me], whole.at[me], whole_send.at[i], whole_recv.at[i], {"graph": p}))
    for copy in copies:
        copy.wait()
    whole_ref[...] = whole[...]


def output_kernel(whole_ref, from_ref, forces_ref, radial_ref, source_ref, out_ref, loss_ref):
    count = radial_ref.shape[0]
    for i in range(whole_ref.shape[0]):
        piece = whole_ref[i].astype(F32)
        for k in range(3):
            at = (3 * i + k) * 8
            if at < count:
                radial_ref[at : at + 8] = piece[8 * k : 8 * k + 8]
            else:
                source_ref[at - count : at - count + 8] = piece[8 * k : 8 * k + 8]
        if i == 0:
            out_ref[...] = piece[24:25] + piece[25:26]
            loss_ref[...] = (piece[26:27] + piece[27:28] + piece[28:29])[:, :1]
    forces_ref[...] = from_ref[...]


def whole_vmem():
    return pl.BlockSpec(memory_space=VMEM)


def local(
    node_state,
    atom_types,
    positions,
    force_ref,
    edge_source,
    edge_count,
    type_table,
    w_rad,
    w_src,
    w_out,
):
    nodes, channels = node_state.shape[1:]
    groups = lax.axis_size("graph")
    batches = lax.axis_size("dp")
    weight_loss = 1.0 / math.sqrt(3.0 * nodes * groups * node_state.shape[0] * batches)
    count = w_rad.shape[0]
    tiles = nodes // LANES
    wide = DEG * LANES
    dma = pltpu.SemaphoreType.DMA

    def shape(*dims, dtype=F32):
        return jax.ShapeDtypeStruct(dims, dtype)

    others = max(batches - 1, 1)
    forces, whole = pl.pallas_call(
        functools.partial(fused_kernel, groups, batches, weight_loss),
        out_shape=(shape(3, 1, nodes), shape(groups, 32, LANES, dtype=BF16)),
        in_specs=[whole_vmem()] * 10,
        out_specs=(whole_vmem(),) * 2,
        scratch_shapes=[
            VMEM((4, channels, nodes), BF16),
            VMEM((4, PAD, LANES), F32),
            VMEM((14 * channels, 256), BF16),
            VMEM((channels, count), BF16),
            VMEM((channels, channels), BF16),
            VMEM((channels, LANES), F32),
            VMEM((count, LANES), F32),
            VMEM((tiles, PAD, LANES), jnp.int32),
            VMEM((tiles, PAD, LANES), jnp.int32),
            VMEM((tiles, 2 * PAD, LANES), F32),
            VMEM((16, LANES), F32),
            VMEM((tiles, 4 * PAD, LANES), F32),
            VMEM((tiles // 2 + 1, 2, count, wide), BF16),
            VMEM((tiles // 2, 2, count, wide), BF16),
            VMEM((tiles, channels, wide), BF16),
            VMEM((tiles, channels, wide), BF16),
            VMEM((tiles, channels, wide), BF16),
            VMEM((tiles, channels, wide), BF16),
            VMEM((tiles, channels, LANES), F32),
            *[VMEM((256, wide), BF16)] * 2,
            *[VMEM((channels, wide), F32)] * 2,
            VMEM((96, 256), F32),
            VMEM((PAD, LANES), F32),
            VMEM((4, PAD, LANES), F32),
            VMEM((3, PAD, LANES), F32),
            VMEM((PAD, LANES), F32),
            VMEM((4, PAD, LANES), F32),
            *[VMEM((channels, wide), BF16)] * 2,
            VMEM((count, channels), F32),
            VMEM((channels, channels), F32),
            VMEM((channels, LANES), F32),
            VMEM((groups, 32, LANES), BF16),
            VMEM((groups - 1, 32, LANES), BF16),
            VMEM((batches, 32, LANES), F32),
            VMEM((groups, 32, LANES), BF16),
            dma((6,)),
            dma((6,)),
            dma((6,)),
            dma((6,)),
            dma((groups - 1,)),
            dma((groups - 1,)),
            dma((others,)),
            dma((others,)),
            dma((groups - 1,)),
            dma((groups - 1,)),
        ],
        compiler_params=pltpu.CompilerParams(
            collective_id=0, has_side_effects=True, vmem_limit_bytes=LIMIT
        ),
        name="fused",
    )(
        node_state[0],
        atom_types,
        positions.transpose(1, 0, 2),
        force_ref.transpose(1, 0, 2),
        edge_source,
        edge_count,
        type_table,
        w_rad,
        w_src,
        w_out.reshape(1, channels),
    )
    forces, grad_radial, grad_source, grad_out, loss = pl.pallas_call(
        output_kernel,
        out_shape=(
            shape(3, 1, nodes),
            shape(count, channels),
            shape(channels, channels),
            shape(1, channels),
            shape(1, 1),
        ),
        in_specs=[whole_vmem()] * 2,
        out_specs=(whole_vmem(),) * 5,
        name="output",
    )(whole, forces)
    return forces.transpose(1, 0, 2), grad_radial, grad_source, grad_out[0], loss[0, 0]


def solution(mesh):
    in_specs = (
        P("dp", "graph", None),
        P("dp", "graph"),
        P("dp", None, "graph"),
        P("dp", None, "graph"),
        P("dp", "graph"),
        P("dp", "graph"),
        P(),
        P(),
        P(),
        P(),
    )
    out_specs = (P("dp", None, "graph"), P(), P(), P(), P())
    return jax.shard_map(local, mesh=mesh, in_specs=in_specs, out_specs=out_specs, check_vma=False)
```

```python
import functools
import math

import jax
import jax.numpy as jnp
from jax import lax
from jax.experimental import pallas as pl
from jax.experimental.pallas import tpu as pltpu
from jax.sharding import PartitionSpec as P

MESH = pl.DeviceIdType.MESH
F32 = jnp.float32
BF16 = jnp.bfloat16
NT = (((1,), (1,)), ((), ()))
DEG = 20
PAD = 24
LANES = 128
VMEM = pltpu.VMEM
LIMIT = 62 * 1024 * 1024
WIDE = DEG * LANES
NEAR = 16


def partners(groups):
    me = lax.axis_index("graph")
    left = lax.rem(me + groups - 1, groups)
    right = lax.rem(me + 1, groups)
    far = lax.rem(me + groups // 2, groups)
    return left, right, far


def farthest_first(count):
    if count == 16:
        return [4, 12, 5, 11, 3, 13, 6, 10, 2, 14, 7, 9, 8, 1, 15]
    if count == 8:
        return [3, 5, 4, 1, 7, 2, 6]
    return list(range(1, count))


def send(src, dst, send_sem, recv_sem, device):
    copy = pltpu.make_async_remote_copy(
        src_ref=src,
        dst_ref=dst,
        send_sem=send_sem,
        recv_sem=recv_sem,
        device_id=device,
        device_id_type=MESH,
    )
    copy.start()
    return copy


def lane_pick(row, index):
    return jnp.take_along_axis(
        jnp.broadcast_to(row, index.shape), index, axis=1, mode="promise_in_bounds"
    )


def pick_three(tab_ref, rows, lane, row_of):
    results = []
    for g in range(0, lane.shape[0], 8):
        lanes_here, row_here = lane[g : g + 8], row_of[g : g + 8]
        result = [jnp.zeros(lanes_here.shape, F32)] * 3
        for r in range(rows):
            here = row_here == r
            for c in range(3):
                at = c * 8 + r % 7
                result[c] = jnp.where(
                    here, lane_pick(tab_ref[r // 7, at : at + 1, :], lanes_here), result[c]
                )
        results.append(result)
    return [jnp.concatenate([result[c] for result in results], axis=0) for c in range(3)]


def basis(dist_row, scaled_centers, gamma):
    diff = (-2.0 * gamma) * dist_row - scaled_centers
    bump = jnp.exp(diff * diff * (-1.0 / (4.0 * gamma)))
    return bump.astype(BF16), (diff * bump).astype(BF16)


def centers(count):
    gamma = count * count / 1152.0
    number = lax.broadcasted_iota(jnp.int32, (count, LANES), 0).astype(F32)
    return number * (12.0 / count) * (-2.0 * gamma), gamma


def node_terms(agg):
    sig = jax.nn.sigmoid(agg)
    first = sig * (1.0 + agg * (1.0 - sig))
    second = sig * (1.0 - sig) * (2.0 + agg * (1.0 - 2.0 * sig))
    return first, second


def prepare_indices(
    groups, source_ref, count_ref, lanes_ref, rows_ref, pick_ref, compact_ref, tiles
):
    me = lax.axis_index("graph")
    slot = lax.broadcasted_iota(jnp.int32, (PAD, LANES), 1) * DEG + lax.broadcasted_iota(
        jnp.int32, (PAD, LANES), 0
    )
    lane = slot & (LANES - 1)
    row_of = slot >> 7
    nodes = tiles * LANES
    for n in range(tiles):
        source = jnp.zeros((PAD, LANES), jnp.int32)
        for r in range(DEG):
            at = (n * DEG + r) * LANES
            source = jnp.where(row_of == r, lane_pick(source_ref[:, at : at + LANES], lane), source)
        block = (source * 74899) >> 26
        offset = (block - me + groups) & (groups - 1)
        position = jnp.where(
            offset == groups - 1, 0, jnp.where(offset == 0, 1, jnp.where(offset == 1, 2, 3))
        )
        picked = position * nodes + source - block * nodes
        live = slot + n * (DEG * LANES) < count_ref[...]
        lanes_ref[n] = picked & (LANES - 1)
        rows_ref[n] = picked >> 7
        pick_ref[n, :PAD] = jnp.where(live, (picked & 255).astype(F32), -1.0)
        pick_ref[n, PAD:] = (picked >> 8).astype(F32)
    lane = lax.broadcasted_iota(jnp.int32, (8, LANES), 1)
    here = (lane >> 4) == lax.broadcasted_iota(jnp.int32, (8, LANES), 0)
    for g in range(2):
        for r in range(PAD // 8):
            values = pick_ref[0, g * PAD + 8 * r : g * PAD + 8 * r + 8]
            values = jnp.take_along_axis(
                values, LANES - NEAR + (lane & (NEAR - 1)), axis=1, mode="promise_in_bounds"
            )
            compact_ref[8 * g + r : 8 * g + r + 1] = jnp.sum(
                jnp.where(here, values, 0.0), axis=0, keepdims=True
            )


def fused_kernel(
    groups,
    batches,
    weight_loss,
    state_ref,
    types_ref,
    place_ref,
    wanted_ref,
    source_ref,
    count_ref,
    table_ref,
    w_rad_ref,
    w_src_ref,
    w_out_ref,
    forces_ref,
    whole_ref,
    states,
    places,
    stack,
    w_rad_t,
    w_src_t,
    w_out_t,
    centre,
    lanes,
    rows_of,
    pick,
    compact,
    scalar,
    basis_a,
    basis_b,
    rows_keep,
    query_keep,
    slope_keep,
    radial_keep,
    agg_keep,
    onehots_a,
    onehots_b,
    product_a,
    product_b,
    spread,
    incoming,
    outgoing,
    terms,
    wanted,
    backs,
    wants_a,
    wants_b,
    grad_radial,
    grad_source,
    grad_out,
    own,
    pieces,
    part,
    whole,
    halo_send,
    halo_recv,
    term_send,
    term_recv,
    piece_send,
    piece_recv,
    part_send,
    part_recv,
    whole_send,
    whole_recv,
):
    nodes, channels = state_ref.shape
    tiles = nodes // LANES
    kinds = table_ref.shape[0]
    count = w_rad_ref.shape[0]
    gamma = count * count / 1152.0
    me = lax.axis_index("graph")
    batch = lax.axis_index("dp")
    left, right, far = partners(groups)
    near_by = (left, right, far)
    peers = [lax.rem(me + d, groups) for d in farthest_first(groups)]
    others = [lax.rem(batch + d, batches) for d in farthest_first(batches)]

    barrier = pltpu.get_barrier_semaphore()
    for device in [{"graph": p} for p in peers] + [{"dp": b} for b in others]:
        pl.semaphore_signal(barrier, inc=1, device_id=device, device_id_type=MESH)

    places[1] = jnp.zeros((PAD, LANES), F32)
    for c in range(3):
        for n in range(tiles):
            at = slice(n * LANES, (n + 1) * LANES)
            places[1, 8 * c + n : 8 * c + n + 1, :] = place_ref[c, :, at]
    pl.semaphore_wait(barrier, len(peers) + len(others))
    targets = ((left, 2), (right, 0), (far, 3))
    place_copies, state_copies = [], []
    for i, (device, slot) in enumerate(targets):
        place_copies.append(
            send(places.at[1], places.at[slot], halo_send.at[i], halo_recv.at[i], {"graph": device})
        )
    kind = (types_ref[...] == lax.broadcasted_iota(jnp.int32, (kinds, nodes), 0)).astype(BF16)
    embedded = lax.dot_general(
        table_ref[...], kind, (((0,), (0,)), ((), ())), preferred_element_type=F32
    )
    states[1] = (state_ref[...].astype(F32).T + embedded).astype(BF16)

    def send_state(i):
        device, slot = targets[i]
        state_copies.append(
            send(
                states.at[1], states.at[slot], halo_send.at[3 + i], halo_recv.at[3 + i], {"graph": device}
            )
        )

    send_state(0)
    send_state(1)

    w_rad_t[...] = w_rad_ref[...].astype(F32).T.astype(BF16)
    w_src_t[...] = w_src_ref[...].astype(F32).T.astype(BF16)
    w_out_t[...] = jnp.broadcast_to(w_out_ref[...], (channels, LANES)).T
    wanted[...] = jnp.zeros_like(wanted)
    for c in range(3):
        for n in range(tiles):
            at = slice(n * LANES, (n + 1) * LANES)
            wanted[8 * c + n : 8 * c + n + 1, :] = wanted_ref[c, :, at]
    centre[...] = centers(count)[0]
    spread[...] = jnp.zeros_like(spread)
    incoming[...] = jnp.zeros_like(incoming)
    grad_radial[...] = jnp.zeros_like(grad_radial)
    grad_source[...] = jnp.zeros_like(grad_source)
    grad_out[...] = jnp.zeros_like(grad_out)
    prepare_indices(groups, source_ref, count_ref, lanes, rows_of, pick, compact, tiles)
    for copy in place_copies:
        copy.wait()
    send_state(2)

    def distances(n, table_rows):
        source_place = pick_three(places, table_rows, lanes[n], rows_of[n])
        delta = [source_place[c] - places[1, pl.ds(8 * c + n, 1), :] for c in range(3)]
        dist = jnp.sqrt(delta[0] * delta[0] + delta[1] * delta[1] + delta[2] * delta[2] + 0.25)
        for c in range(3):
            scalar[n, c * PAD : (c + 1) * PAD] = delta[c] / dist
        scalar[n, 3 * PAD :] = dist

    def bases(n, kept):
        for j in range(DEG):
            at = slice(j * LANES, (j + 1) * LANES)
            bump, slant = basis(scalar[n, 3 * PAD + j : 3 * PAD + j + 1, :], centre[...], gamma)
            kept[0, :, at] = bump
            kept[1, :, at] = slant

    def stack_up(halves):
        for half in halves:
            at = (half % 7) * LANES
            stack[
                (half // 2) * channels : (half // 2 + 1) * channels,
                (half % 2) * LANES : (half % 2 + 1) * LANES,
            ] = states[half // 7, :, at : at + LANES]

    def three_distances(i, unused):
        for k in range(1, 4):
            distances(3 * i + k, 21)
        return unused

    lax.fori_loop(0, (tiles - 1) // 3, three_distances, 0)
    distances(0, 28)

    def ahead(i, unused):
        bases(2 * i + 1, basis_a.at[i])
        bases(2 * i + 2, basis_b.at[i])
        return unused

    lax.fori_loop(0, tiles // 2, ahead, 0)
    bases(0, basis_a.at[tiles // 2])
    stack[10 * channels : 11 * channels, LANES:] = jnp.zeros((channels, LANES), BF16)
    for copy in state_copies[:2]:
        copy.wait()
    stack_up(range(21))

    numbers = lax.broadcasted_iota(jnp.int32, (256, LANES), 0).astype(F32)

    def look_up(columns, chosen, first, last):
        ones = jnp.concatenate([(numbers == column).astype(BF16) for column in columns], axis=1)
        hi = jnp.concatenate(chosen, axis=1)
        hi = jnp.broadcast_to(hi, (channels, hi.shape[1]))
        found = jnp.dot(
            stack[first * channels : last * channels], ones, preferred_element_type=F32
        )
        rows = found[:channels]
        for c in range(1, last - first):
            rows = jnp.where(
                hi == float(first + c), found[c * channels : (c + 1) * channels], rows
            )
        return ones, rows

    def gather(n, kept, onehots, product):
        columns = [pick[n, pl.ds(j, 1), :] for j in range(DEG)]
        chosen = [pick[n, pl.ds(PAD + j, 1), :] for j in range(DEG)]
        if isinstance(n, int):
            ones, rows = look_up(columns, chosen, 10, 14)
            _, near = look_up(
                [compact[r : r + 1] for r in range(3)], [compact[8 + r : 9 + r] for r in range(3)], 0, 11
            )
            last = lax.broadcasted_iota(jnp.int32, (channels, LANES), 1) >= LANES - NEAR
            parts = []
            for j in range(DEG):
                moved = pltpu.roll(
                    near[:, (j // 8) * LANES : (j // 8 + 1) * LANES],
                    LANES - NEAR - NEAR * (j % 8),
                    1,
                )
                parts.append(jnp.where(last, moved, rows[:, j * LANES : (j + 1) * LANES]))
            rows = jnp.concatenate(parts, axis=1)
        else:
            ones, rows = look_up(columns, chosen, 0, 11)
        onehots[...] = ones
        rows = rows.astype(BF16)
        rows_keep[n] = rows
        query = jnp.dot(w_src_t[...], rows, preferred_element_type=F32)
        radial = jnp.dot(w_rad_t[...], kept[0], preferred_element_type=F32)
        slope = jnp.dot(w_rad_t[...], kept[1], preferred_element_type=F32)
        query_keep[n] = query.astype(BF16)
        slope_keep[n] = slope.astype(BF16)
        radial_keep[n] = radial.astype(BF16)
        product[...] = query * slope
        term = radial * query
        total = term[:, :LANES]
        for j in range(1, DEG):
            total = total + term[:, j * LANES : (j + 1) * LANES]
        agg_keep[n] = 0.2 * total

    def pull(n, onehots, product):
        first, _ = node_terms(agg_keep[n])
        readout = 0.2 * first * w_out_t[...]
        inward = [jnp.zeros((1, LANES), F32)] * 3
        lhs = []
        chunk = lax.broadcasted_iota(jnp.int32, (16, LANES), 0).astype(F32)
        for j in range(DEG):
            force = jnp.sum(readout * product[:, j * LANES : (j + 1) * LANES], axis=0, keepdims=True)
            here = chunk == pick[n, PAD + j : PAD + j + 1, :]
            high, low = [], []
            for c in range(3):
                moved = force * scalar[n, c * PAD + j : c * PAD + j + 1, :]
                inward[c] = inward[c] + moved
                term = jnp.where(here, moved, 0.0)
                top = term.astype(BF16)
                high.append(top)
                low.append((term - top.astype(F32)).astype(BF16))
            lhs.append(jnp.concatenate(high + low, axis=0))
        lhs = jnp.concatenate(lhs, axis=1)
        spread[...] += lax.dot_general(lhs, onehots[...], NT, preferred_element_type=F32)
        for c in range(3):
            incoming[pl.ds(8 * c + n, 1), :] = inward[c]

    def two_forward(i, unused):
        n = 2 * i + 1
        pull(n, onehots_a, product_a)
        gather(n + 1, basis_b.at[i], onehots_b, product_b)
        pull(n + 1, onehots_b, product_b)
        gather(n + 2, basis_a.at[i + 1], onehots_a, product_a)
        return unused

    gather(jnp.int32(1), basis_a.at[0], onehots_a, product_a)
    lax.fori_loop(0, (tiles - 3) // 2, two_forward, 0)
    pull(tiles - 2, onehots_a, product_a)
    gather(jnp.int32(tiles - 1), basis_b.at[tiles // 2 - 1], onehots_b, product_b)
    state_copies[2].wait()
    stack_up(range(21, 28))
    pull(tiles - 1, onehots_b, product_b)
    gather(0, basis_a.at[tiles // 2], onehots_a, product_a)
    pull(0, onehots_a, product_a)

    outgoing[...] = jnp.zeros_like(outgoing)
    total = spread[:48] + spread[48:]
    for c in range(3):
        for r in range(28):
            at = c * 8 + r % 7
            outgoing[r // 7, at : at + 1, :] = total[
                c * 16 + r // 2 : c * 16 + r // 2 + 1, (r % 2) * LANES : (r % 2 + 1) * LANES
            ]
    copies = []
    for i, (device, slot) in enumerate(((left, 0), (right, 2), (far, 3))):
        copies.append(
            send(outgoing.at[slot], terms.at[i], term_send.at[i], term_recv.at[i], {"graph": device})
        )
    for copy in copies:
        copy.wait()
    forces = incoming[...] - (outgoing[1] + terms[0] + terms[1] + terms[2])
    miss = forces - wanted[...]
    backs[1] = 2.0 * weight_loss * miss
    copies = []
    for i, (device, slot) in enumerate(((left, 2), (right, 0), (far, 3))):
        copies.append(
            send(backs.at[1], backs.at[slot], term_send.at[3 + i], term_recv.at[3 + i], {"graph": device})
        )
    for c in range(3):
        for n in range(tiles):
            forces_ref[c, :, n * LANES : (n + 1) * LANES] = forces[8 * c + n : 8 * c + n + 1, :]
    loss = weight_loss * jnp.sum(miss * miss, axis=(0, 1), keepdims=True)
    for copy in copies:
        copy.wait()

    def coefficients(n, table_rows, plain_coef, slope_coef, wants):
        source_back = pick_three(backs, table_rows, lanes[n], rows_of[n])
        lam = jnp.zeros((PAD, LANES), F32)
        for c in range(3):
            lam = lam + (backs[1, pl.ds(8 * c + n, 1), :] - source_back[c]) * scalar[
                n, c * PAD : (c + 1) * PAD
            ]
        lam = 0.2 * lam
        first, second = node_terms(agg_keep[n])
        w_out = w_out_t[...]
        readout = first * w_out
        dread = jnp.zeros((channels, LANES), F32)
        for j in range(DEG):
            at = slice(j * LANES, (j + 1) * LANES)
            dread = dread + lam[j : j + 1] * (
                query_keep[n, :, at].astype(F32) * slope_keep[n, :, at].astype(F32)
            )
        grad_out[...] += dread * first
        plain = 0.2 * dread * w_out * second
        for j in range(DEG):
            at = slice(j * LANES, (j + 1) * LANES)
            over_slope = lam[j : j + 1] * readout
            query = query_keep[n, :, at].astype(F32)
            plain_coef[:, at] = (plain * query).astype(BF16)
            slope_coef[:, at] = (over_slope * query).astype(BF16)
            wants[:, at] = (
                over_slope * slope_keep[n, :, at].astype(F32)
                + plain * radial_keep[n, :, at].astype(F32)
            ).astype(BF16)

    def products(n, kept, plain_coef, slope_coef, wants):
        grad_radial[...] += lax.dot_general(
            kept[0], plain_coef[...], NT, preferred_element_type=F32
        ) + lax.dot_general(kept[1], slope_coef[...], NT, preferred_element_type=F32)
        grad_source[...] += lax.dot_general(
            rows_keep[n], wants[...], NT, preferred_element_type=F32
        )

    coef_a = (onehots_a.at[:channels], onehots_a.at[channels : 2 * channels], wants_a)
    coef_b = (onehots_b.at[:channels], onehots_b.at[channels : 2 * channels], wants_b)
    def two_backward(i, unused):
        n = 2 * i + 1
        products(n, basis_a.at[i], *coef_a)
        coefficients(n + 1, 21, *coef_b)
        products(n + 1, basis_b.at[i], *coef_b)
        coefficients(n + 2, 21, *coef_a)
        return unused

    coefficients(1, 21, *coef_a)
    lax.fori_loop(0, (tiles - 3) // 2, two_backward, 0)
    products(tiles - 2, basis_a.at[tiles // 2 - 1], *coef_a)
    coefficients(tiles - 1, 21, *coef_b)
    products(tiles - 1, basis_b.at[tiles // 2 - 1], *coef_b)
    coefficients(0, 28, *coef_a)
    products(0, basis_a.at[tiles // 2], *coef_a)

    def parts_of(value, number):
        parts = []
        for _ in range(number):
            part = value.astype(BF16).astype(F32)
            parts.append(part)
            value = value - part
        return parts

    def piece_of(rows, out, loss):
        more = parts_of(out, 2) + parts_of(loss, 3) + [jnp.zeros((3, LANES), F32)]
        return jnp.concatenate([rows] + more, axis=0)

    radial = grad_radial[...]
    source = grad_source[...]
    nothing = jnp.zeros((1, LANES), F32)
    for i in range(groups):
        rows = [
            radial[at : at + 8] if at < count else source[at - count : at - count + 8]
            for at in range(24 * i, 24 * i + 24, 8)
        ]
        out = nothing if i else jnp.sum(grad_out[...].T, axis=0, keepdims=True)
        total = nothing if i else jnp.broadcast_to(loss, (1, LANES))
        own[i] = piece_of(jnp.concatenate(rows, axis=0), out, total).astype(BF16)
    copies = []
    for i, p in enumerate(peers):
        copies.append(send(own.at[p], pieces.at[i], piece_send.at[i], piece_recv.at[i], {"graph": p}))
    for copy in copies:
        copy.wait()
    total = own[me].astype(F32)
    for i in range(groups - 1):
        total = total + pieces[i].astype(F32)
    part[batch] = total
    copies = []
    for i, b in enumerate(others):
        copies.append(send(part.at[batch], part.at[batch], part_send.at[i], part_recv.at[i], {"dp": b}))
    for copy in copies:
        copy.wait()
    total = part[0]
    for i in range(1, batches):
        total = total + part[i]
    whole[me] = piece_of(
        total[:24], total[24:25] + total[25:26], total[26:27] + total[27:28] + total[28:29]
    ).astype(BF16)
    copies = []
    for i, p in enumerate(peers):
        copies.append(send(whole.at[me], whole.at[me], whole_send.at[i], whole_recv.at[i], {"graph": p}))
    for copy in copies:
        copy.wait()
    whole_ref[...] = whole[...]


def output_kernel(whole_ref, from_ref, forces_ref, radial_ref, source_ref, out_ref, loss_ref):
    count = radial_ref.shape[0]
    for i in range(whole_ref.shape[0]):
        piece = whole_ref[i].astype(F32)
        for k in range(3):
            at = (3 * i + k) * 8
            if at < count:
                radial_ref[at : at + 8] = piece[8 * k : 8 * k + 8]
            else:
                source_ref[at - count : at - count + 8] = piece[8 * k : 8 * k + 8]
        if i == 0:
            out_ref[...] = piece[24:25] + piece[25:26]
            loss_ref[...] = (piece[26:27] + piece[27:28] + piece[28:29])[:, :1]
    forces_ref[...] = from_ref[...]


def whole_vmem():
    return pl.BlockSpec(memory_space=VMEM)


def local(
    node_state,
    atom_types,
    positions,
    force_ref,
    edge_source,
    edge_count,
    type_table,
    w_rad,
    w_src,
    w_out,
):
    nodes, channels = node_state.shape[1:]
    groups = lax.axis_size("graph")
    batches = lax.axis_size("dp")
    weight_loss = 1.0 / math.sqrt(3.0 * nodes * groups * node_state.shape[0] * batches)
    count = w_rad.shape[0]
    tiles = nodes // LANES
    wide = DEG * LANES
    dma = pltpu.SemaphoreType.DMA

    def shape(*dims, dtype=F32):
        return jax.ShapeDtypeStruct(dims, dtype)

    others = max(batches - 1, 1)
    forces, whole = pl.pallas_call(
        functools.partial(fused_kernel, groups, batches, weight_loss),
        out_shape=(shape(3, 1, nodes), shape(groups, 32, LANES, dtype=BF16)),
        in_specs=[whole_vmem()] * 10,
        out_specs=(whole_vmem(),) * 2,
        scratch_shapes=[
            VMEM((4, channels, nodes), BF16),
            VMEM((4, PAD, LANES), F32),
            VMEM((14 * channels, 256), BF16),
            VMEM((channels, count), BF16),
            VMEM((channels, channels), BF16),
            VMEM((channels, LANES), F32),
            VMEM((count, LANES), F32),
            VMEM((tiles, PAD, LANES), jnp.int32),
            VMEM((tiles, PAD, LANES), jnp.int32),
            VMEM((tiles, 2 * PAD, LANES), F32),
            VMEM((16, LANES), F32),
            VMEM((tiles, 4 * PAD, LANES), F32),
            VMEM((tiles // 2 + 1, 2, count, wide), BF16),
            VMEM((tiles // 2, 2, count, wide), BF16),
            VMEM((tiles, channels, wide), BF16),
            VMEM((tiles, channels, wide), BF16),
            VMEM((tiles, channels, wide), BF16),
            VMEM((tiles, channels, wide), BF16),
            VMEM((tiles, channels, LANES), F32),
            *[VMEM((256, wide), BF16)] * 2,
            *[VMEM((channels, wide), F32)] * 2,
            VMEM((96, 256), F32),
            VMEM((PAD, LANES), F32),
            VMEM((4, PAD, LANES), F32),
            VMEM((3, PAD, LANES), F32),
            VMEM((PAD, LANES), F32),
            VMEM((4, PAD, LANES), F32),
            *[VMEM((channels, wide), BF16)] * 2,
            VMEM((count, channels), F32),
            VMEM((channels, channels), F32),
            VMEM((channels, LANES), F32),
            VMEM((groups, 32, LANES), BF16),
            VMEM((groups - 1, 32, LANES), BF16),
            VMEM((batches, 32, LANES), F32),
            VMEM((groups, 32, LANES), BF16),
            dma((6,)),
            dma((6,)),
            dma((6,)),
            dma((6,)),
            dma((groups - 1,)),
            dma((groups - 1,)),
            dma((others,)),
            dma((others,)),
            dma((groups - 1,)),
            dma((groups - 1,)),
        ],
        compiler_params=pltpu.CompilerParams(
            collective_id=0, has_side_effects=True, vmem_limit_bytes=LIMIT
        ),
        name="fused",
    )(
        node_state[0],
        atom_types,
        positions.transpose(1, 0, 2),
        force_ref.transpose(1, 0, 2),
        edge_source,
        edge_count,
        type_table,
        w_rad,
        w_src,
        w_out.reshape(1, channels),
    )
    forces, grad_radial, grad_source, grad_out, loss = pl.pallas_call(
        output_kernel,
        out_shape=(
            shape(3, 1, nodes),
            shape(count, channels),
            shape(channels, channels),
            shape(1, channels),
            shape(1, 1),
        ),
        in_specs=[whole_vmem()] * 2,
        out_specs=(whole_vmem(),) * 5,
        name="output",
    )(whole, forces)
    return forces.transpose(1, 0, 2), grad_radial, grad_source, grad_out[0], loss[0, 0]


def solution(mesh):
    in_specs = (
        P("dp", "graph", None),
        P("dp", "graph"),
        P("dp", None, "graph"),
        P("dp", None, "graph"),
        P("dp", "graph"),
        P("dp", "graph"),
        P(),
        P(),
        P(),
        P(),
    )
    out_specs = (P("dp", None, "graph"), P(), P(), P(), P())
    return jax.shard_map(local, mesh=mesh, in_specs=in_specs, out_specs=out_specs, check_vma=False)
```
